32 devices in a mesh: dp: 8 (over z, y), row: 2 (over x), col: 2 (over core).
Axes of the slice: x: 2, y: 2, z: 4, core: 2. Of those that a mesh axis runs over, the one named last changes fastest.
Arguments:
- latents: bfloat16 [8192, 1152], P('dp', ('row', 'col')), may hold values from -6 to 6
- text: bfloat16 [8, 120, 4096], P('dp', None, ('row', 'col')), may hold values from -6 to 6
- text_len: int32 [8], replicated, may hold values from 1 to 120
- time_ids: int32 [8], replicated, may hold values from 0 to 15
- time_table: float32 [16, 6, 1152], P(None, None, ('row', 'col')), may hold values from -4 to 4
- shift_table: float32 [6, 1152], P(None, ('row', 'col')), may hold values from -4 to 4
- w_qkv: bfloat16 [1152, 3, 1152], P('row', None, 'col'), may hold values from -0.1875 to 0.1875
- b_qv: float32 [2, 1152], P(None, ('col', 'row')), may hold values from -3 to 3
- w_out: bfloat16 [1152, 1152], P('col', 'row'), may hold values from -0.75 to 0.75
- b_out: float32 [1152], P(('row', 'col')), may hold values from -3 to 3
- w_cross_q: bfloat16 [1152, 1152], P('row', 'col'), may hold values from -0.1875 to 0.1875
- b_cross_q: float32 [1152], P(('col', 'row')), may hold values from -3 to 3
- w_cross_kv: bfloat16 [4096, 2, 1152], P('row', None, 'col'), may hold values from -0.09375 to 0.09375
- b_cross_v: float32 [1152], P(('col', 'row')), may hold values from -3 to 3
- w_cross_out: bfloat16 [1152, 1152], P('col', 'row'), may hold values from -0.375 to 0.375
- b_cross_out: float32 [1152], P(('row', 'col')), may hold values from -3 to 3
- w_fc1: bfloat16 [1152, 4608], P('row', 'col'), may hold values from -0.1875 to 0.1875
- b_fc1: float32 [4608], P(('col', 'row')), may hold values from -3 to 3
- w_fc2: bfloat16 [4608, 1152], P('col', 'row'), may hold values from -0.09375 to 0.09375
- b_fc2: float32 [1152], P(('row', 'col')), may hold values from -3 to 3
- grad_out: bfloat16 [8192, 1152], P('dp', ('row', 'col')), may hold values from -6 to 6
Outputs:
- out: bfloat16 [8192, 1152], P('dp', ('row', 'col'))
- grad_latents: float32 [8192, 1152], P('dp', ('row', 'col'))
- grad_text: float32 [8, 120, 4096], P('dp', None, ('row', 'col'))
- grad_time_table: float32 [16, 6, 1152], P(None, None, ('row', 'col'))
- grad_shift_table: float32 [6, 1152], P(None, ('row', 'col'))
- grad_w_qkv: float32 [1152, 3, 1152], P(('row', 'dp'), None, 'col')
- grad_b_qv: float32 [2, 1152], P(None, ('col', 'row'))
- grad_w_out: float32 [1152, 1152], P(('col', 'dp'), 'row')
- grad_b_out: float32 [1152], P(('row', 'col'))
- grad_w_cross_q: float32 [1152, 1152], P(('row', 'dp'), 'col')
- grad_b_cross_q: float32 [1152], P(('col', 'row'))
- grad_w_cross_kv: float32 [4096, 2, 1152], P(('row', 'dp'), None, 'col')
- grad_b_cross_v: float32 [1152], P(('col', 'row'))
- grad_w_cross_out: float32 [1152, 1152], P(('col', 'dp'), 'row')
- grad_b_cross_out: float32 [1152], P(('row', 'col'))
- grad_w_fc1: float32 [1152, 4608], P(('row', 'dp'), 'col')
- grad_b_fc1: float32 [4608], P(('col', 'row'))
- grad_w_fc2: float32 [4608, 1152], P(('col', 'dp'), 'row')
- grad_b_fc2: float32 [1152], P(('row', 'col'))
The draws below stay inside these ranges and needn't reach their ends.
All inputs are finite; a program needn't handle non-finite values.
Results may differ from the reference program's by a relative error of at most 0.018.
Values may be sent and summed in bfloat16 or wider, within the bound.
No kernel may reach another device: no remote copies, remote signals or barrier semaphores. Data moves between devices by JAX's collectives and lax.ppermute only.
A program may use at most 256 MiB of HBM per device.

```python
from functools import partial
import jax
import jax.numpy as jnp
from jax import lax

MODEL_WIDTH = 1152
HEADS = 16
HD = 72
FF = 4608
TXT_DIM = 4096
TXT = 120
NTAB = 16
SEQ_DEV = 512
LPP = 2
LATENTS = 8
TOKENS = 8192
N_DP = 8


def plant(drawn, stream_key, low, largest):
    longest = drawn.shape.index(max(drawn.shape))
    spots = []
    for shift in (0, 1):
        where = [jax.random.randint(jax.random.fold_in(stream_key, axis), (), 0, length) for axis, length in enumerate(drawn.shape)]
        where[longest] = (where[longest] + shift) % drawn.shape[longest]
        spots.append(tuple(where))
    return drawn.at[spots[0]].set(low).at[spots[1]].set(largest)


def level_of(rng, dims, pieces, smallest, largest):
    level, own = 1.0, jax.random.fold_in(rng, 6)
    for dim, blocks in pieces:
        steps = jnp.exp(jax.random.uniform(jax.random.fold_in(own, dim), (blocks,), jnp.float32, smallest / len(pieces), largest / len(pieces)))
        level = level * jnp.repeat(steps, dims[dim] // blocks).reshape([-1 if axis == dim else 1 for axis in range(len(dims))])
    return level


def centred(rng, extent, spread, most, cuts=(), dtype=jnp.bfloat16):
    values = jax.random.normal(rng, extent, jnp.float32) * spread
    if len(cuts) > 0:
        values = level_of(rng, extent, cuts, -0.22, 0.18) * values
    return jnp.clip(values, min=-most, max=most).astype(dtype)


def setup_inputs(seed: int = 0) -> dict:
    keys = jax.random.split(jax.random.key(seed), 22)
    return {
        "latents": centred(keys[0], (TOKENS, MODEL_WIDTH), 1.0, 6.0, ((0, 8), (1, 4))),
        "text": centred(keys[1], (LATENTS, TXT, TXT_DIM), 1.0, 6.0, ((0, 8), (2, 4))),
        "text_len": plant(jax.random.randint(keys[2], (LATENTS,), 1, TXT + 1), jax.random.fold_in(keys[2], 1), 1, TXT).astype(jnp.int32),
        "time_ids": plant(jax.random.randint(keys[3], (LATENTS,), 0, NTAB), jax.random.fold_in(keys[3], 1), 0, NTAB - 1).astype(jnp.int32),
        "time_table": centred(keys[4], (NTAB, 6, MODEL_WIDTH), 0.4, 4.0, ((2, 4),), jnp.float32),
        "shift_table": centred(keys[5], (6, MODEL_WIDTH), 0.4, 4.0, ((1, 4),), jnp.float32),
        "w_qkv": centred(keys[6], (MODEL_WIDTH, 3, MODEL_WIDTH), MODEL_WIDTH ** -0.5, 0.1875, ((0, 2), (2, 2))),
        "b_qv": centred(keys[7], (2, MODEL_WIDTH), 0.3, 3.0, ((1, 4),), jnp.float32),
        "w_out": centred(keys[8], (MODEL_WIDTH, MODEL_WIDTH), (MODEL_WIDTH // 16) ** -0.5, 0.75, ((0, 2), (1, 2))),
        "b_out": centred(keys[9], (MODEL_WIDTH,), 0.3, 3.0, ((0, 4),), jnp.float32),
        "w_cross_q": centred(keys[10], (MODEL_WIDTH, MODEL_WIDTH), MODEL_WIDTH ** -0.5, 0.1875, ((0, 2), (1, 2))),
        "b_cross_q": centred(keys[11], (MODEL_WIDTH,), 0.3, 3.0, ((0, 4),), jnp.float32),
        "w_cross_kv": centred(keys[12], (TXT_DIM, 2, MODEL_WIDTH), TXT_DIM ** -0.5, 0.09375, ((0, 2), (2, 2))),
        "b_cross_v": centred(keys[13], (MODEL_WIDTH,), 0.3, 3.0, ((0, 4),), jnp.float32),
        "w_cross_out": centred(keys[14], (MODEL_WIDTH, MODEL_WIDTH), (MODEL_WIDTH // 4) ** -0.5, 0.375, ((0, 2), (1, 2))),
        "b_cross_out": centred(keys[15], (MODEL_WIDTH,), 0.3, 3.0, ((0, 4),), jnp.float32),
        "w_fc1": centred(keys[16], (MODEL_WIDTH, FF), MODEL_WIDTH ** -0.5, 0.1875, ((0, 2), (1, 2))),
        "b_fc1": centred(keys[17], (FF,), 0.3, 3.0, ((0, 4),), jnp.float32),
        "w_fc2": centred(keys[18], (FF, MODEL_WIDTH), FF ** -0.5, 0.09375, ((0, 2), (1, 2))),
        "b_fc2": centred(keys[19], (MODEL_WIDTH,), 0.3, 3.0, ((0, 4),), jnp.float32),
        "grad_out": centred(keys[20], (TOKENS, MODEL_WIDTH), 1.0, 6.0, ((0, 8), (1, 4))),
    }


@jax.custom_vjp
def reduced_precision(v):
    return lax.optimization_barrier(v.astype(jnp.bfloat16)).astype(jnp.float32)

@jax.custom_vjp
def low_back(v):
    return v

def low_keep(v):
    return (reduced_precision(v), None)

def low_pass(kept, grad):
    return (grad,)

def back_keep(v):
    return (v, None)

def back_low(kept, grad):
    return (reduced_precision(grad),)
reduced_precision.defvjp(low_keep, low_pass)
low_back.defvjp(back_keep, back_low)
norm_eps = 1e-06
masked_score = -1000000000.0

def product(left_side, right_side):
    return jnp.tensordot(left_side, right_side, axes=1, precision=lax.Precision.HIGHEST)

def layer_normalize(residual_state):
    center = residual_state - lax.optimization_barrier(jnp.mean(residual_state, axis=-1, keepdims=True))
    return center * lax.rsqrt(lax.optimization_barrier(jnp.mean(center * center, axis=-1, keepdims=True)) + norm_eps)

def attend(queries, key_rows, value_rows, key_valid):
    score_scale = HD ** (-0.5)
    scores = jnp.einsum('qhd,khd->hqk', queries, key_rows, precision=lax.Precision.HIGHEST) * score_scale
    scores = low_back(scores)
    scores = jnp.where(key_valid[None, None, :], scores, masked_score)
    weights = reduced_precision(jax.nn.softmax(scores, axis=-1))
    mixture = jnp.einsum('hqk,khd->qhd', weights, value_rows, precision=lax.Precision.HIGHEST)
    return reduced_precision(low_back(mixture.reshape(mixture.shape[0], MODEL_WIDTH)))

def latent_layer(params, latent_state, caption, modulation_vectors, length):
    w_qkv, b_qv, w_out, b_out, w_cross_q, b_cross_q, w_cross_kv, b_cross_v, w_cross_out, b_cross_out, w_fc1, b_fc1, w_fc2, b_fc2 = params
    self_attention_offset, self_attention_scale, self_attention_gate, feedforward_offset, feedforward_scale, feedforward_gate = modulation_vectors
    tokens_here = latent_state.shape[0]
    normalized_rows = reduced_precision(layer_normalize(latent_state) * (1.0 + self_attention_scale) + self_attention_offset)
    joined_qkv = low_back(product(normalized_rows, w_qkv))
    queries = reduced_precision(joined_qkv[:, 0] + b_qv[0]).reshape(tokens_here, HEADS, HD)
    key_rows = reduced_precision(joined_qkv[:, 1]).reshape(tokens_here, HEADS, HD)
    value_rows = reduced_precision(joined_qkv[:, 2] + b_qv[1]).reshape(tokens_here, HEADS, HD)
    every_key = jnp.ones((tokens_here,), jnp.bool_)
    attended = attend(queries, key_rows, value_rows, every_key)
    residual_branch = low_back(product(attended, w_out)) + b_out
    post_self_attention = latent_state + self_attention_gate * residual_branch
    cross_queries = reduced_precision(low_back(product(reduced_precision(post_self_attention), w_cross_q)) + b_cross_q).reshape(tokens_here, HEADS, HD)
    text_kv = low_back(product(reduced_precision(caption), w_cross_kv))
    cross_keys = reduced_precision(text_kv[:, 0]).reshape(TXT, HEADS, HD)
    cross_values = reduced_precision(text_kv[:, 1] + b_cross_v).reshape(TXT, HEADS, HD)
    key_valid = jnp.arange(TXT) < length
    crossed = attend(cross_queries, cross_keys, cross_values, key_valid)
    after_cross = post_self_attention + low_back(product(crossed, w_cross_out)) + b_cross_out
    normed_two = reduced_precision(layer_normalize(after_cross) * (1.0 + feedforward_scale) + feedforward_offset)
    hidden = low_back(product(normed_two, w_fc1)) + b_fc1
    activated = reduced_precision(jax.nn.gelu(hidden, approximate=True))
    return after_cross + feedforward_gate * (low_back(product(activated, w_fc2)) + b_fc2)

def reference(latents, text, text_len, time_ids, time_table, shift_table, w_qkv, b_qv, w_out, b_out, w_cross_q, b_cross_q, w_cross_kv, b_cross_v, w_cross_out, b_cross_out, w_fc1, b_fc1, w_fc2, b_fc2, grad_out):
    pair_count = N_DP // 2

    def forward(latent_in, caption_in, table_in, shift_in, params):
        grouped = latent_in.reshape(pair_count, 2, LPP, SEQ_DEV, MODEL_WIDTH).transpose(0, 2, 1, 3, 4).reshape(LATENTS, 2 * SEQ_DEV, MODEL_WIDTH)
        modulations = shift_in[None] + table_in[time_ids]
        checked = jax.checkpoint(partial(latent_layer, params))
        result = lax.map(lambda packed: checked(packed[0], packed[1], packed[2], packed[3]), (grouped, caption_in, modulations, text_len))
        return result.reshape(pair_count, LPP, 2, SEQ_DEV, MODEL_WIDTH).transpose(0, 2, 1, 3, 4).reshape(TOKENS, MODEL_WIDTH)
    float_params = tuple((weight.astype(jnp.float32) for weight in (w_qkv, b_qv, w_out, b_out, w_cross_q, b_cross_q, w_cross_kv, b_cross_v, w_cross_out, b_cross_out, w_fc1, b_fc1, w_fc2, b_fc2)))
    output, pullback = jax.vjp(forward, latents.astype(jnp.float32), text.astype(jnp.float32), time_table, shift_table, float_params)
    grad_latents, grad_text, grad_table, grad_shift, grad_params = pullback(grad_out.astype(jnp.float32))
    return (output.astype(jnp.bfloat16), grad_latents, grad_text, grad_table, grad_shift, grad_params[0], grad_params[1], grad_params[2], grad_params[3], grad_params[4], grad_params[5], grad_params[6], grad_params[7], grad_params[8], grad_params[9], grad_params[10], grad_params[11], grad_params[12], grad_params[13])
```

```python
from functools import partial

import jax
import jax.numpy as jnp
from jax import lax
from jax.experimental import pallas as pl
from jax.experimental.pallas import tpu as pltpu
from jax.sharding import PartitionSpec as P

HD = 72
TXT = 120
TXT_PAD = 128
SEQ_DEV = 512
LPP = 2
HALF = 256

norm_eps = 1e-06
masked_score = -1000000000.0
f32 = jnp.float32
bf16 = jnp.bfloat16


def swap(value, axis):
    return lax.ppermute(value, axis, [(0, 1), (1, 0)])


def swap_dp(value, bit):
    return lax.ppermute(value, "dp", [(i, i ^ (1 << bit)) for i in range(lax.axis_size("dp"))])


def pick(pair_first, pair_second, index):
    return jnp.where(index == 0, pair_first, pair_second)


def in_order(mine, other, index, axis):
    return jnp.concatenate([pick(mine, other, index), pick(other, mine, index)], axis=axis)


def after(value, *earlier):
    return lax.optimization_barrier((value, *earlier))[0]


def dot(left, right, left_dim, right_dim):
    return lax.dot_general(
        left, right, (((left_dim,), (right_dim,)), ((), ())), preferred_element_type=f32
    )


def attend_kernel(masked, length_ref, q_ref, k_ref, v_ref, o_ref, log_ref):
    q, k, v = q_ref[0], k_ref[0], v_ref[0]
    scores = dot(k, q, 0, 0) * (HD ** (-0.5))
    if masked:
        place = lax.broadcasted_iota(jnp.int32, scores.shape, 0)
        scores = jnp.where(place < length_ref[0], scores, masked_score)
    largest = jnp.max(scores, axis=0, keepdims=True)
    raised = jnp.exp(scores - largest)
    total = jnp.sum(raised, axis=0, keepdims=True)
    mixture = dot(v, raised.astype(bf16), 1, 0)
    o_ref[0] = (mixture / total).astype(bf16)
    log_ref[0] = largest + jnp.log(total)


def attend(q, k, v, length, masked):
    heads, hd, nq = q.shape
    nk = k.shape[2]
    head = lambda h: (h, 0, 0)
    return pl.pallas_call(
        partial(attend_kernel, masked),
        grid=(heads,),
        in_specs=[
            pl.BlockSpec(memory_space=pltpu.SMEM),
            pl.BlockSpec((1, hd, nq), head),
            pl.BlockSpec((1, hd, nk), head),
            pl.BlockSpec((1, hd, nk), head),
        ],
        out_specs=[pl.BlockSpec((1, hd, nq), head), pl.BlockSpec((1, 1, nq), head)],
        out_shape=[
            jax.ShapeDtypeStruct((heads, hd, nq), bf16),
            jax.ShapeDtypeStruct((heads, 1, nq), f32),
        ],
        compiler_params=pltpu.CompilerParams(vmem_limit_bytes=32 * 2**20),
        cost_estimate=pl.CostEstimate(
            flops=4 * heads * nq * nk * 128,
            bytes_accessed=4 * heads * hd * (nq + nk),
            transcendentals=heads * nq * nk,
        ),
        name="attend_fwd",
    )(length, q, k, v)


def attend_grad_kernel(
    masked, length_ref, q_ref, k_ref, v_ref, g_ref, log_ref, dq_ref, dk_ref, dv_ref
):
    q, k, v, g = q_ref[0], k_ref[0], v_ref[0], g_ref[0]
    scores = dot(k, q, 0, 0) * (HD ** (-0.5))
    if masked:
        place = lax.broadcasted_iota(jnp.int32, scores.shape, 0)
        scores = jnp.where(place < length_ref[0], scores, masked_score)
    weights = jnp.exp(scores - log_ref[0])
    grad_weights = dot(v, g, 0, 0)
    crossed = jnp.sum(grad_weights * weights, axis=0, keepdims=True)
    grad_scores = (weights * (grad_weights - crossed)).astype(bf16)
    dq_ref[0] = (dot(k, grad_scores, 1, 0) * (HD ** (-0.5))).astype(bf16)
    dk_ref[0] = (dot(q, grad_scores, 1, 1) * (HD ** (-0.5))).astype(bf16)
    dv_ref[0] = dot(g, weights.astype(bf16), 1, 1).astype(bf16)


def attend_grad(q, k, v, g, log_total, length, masked):
    heads, hd, nq = q.shape
    nk = k.shape[2]
    head = lambda h: (h, 0, 0)
    return pl.pallas_call(
        partial(attend_grad_kernel, masked),
        grid=(heads,),
        in_specs=[
            pl.BlockSpec(memory_space=pltpu.SMEM),
            pl.BlockSpec((1, hd, nq), head),
            pl.BlockSpec((1, hd, nk), head),
            pl.BlockSpec((1, hd, nk), head),
            pl.BlockSpec((1, hd, nq), head),
            pl.BlockSpec((1, 1, nq), head),
        ],
        out_specs=[
            pl.BlockSpec((1, hd, nq), head),
            pl.BlockSpec((1, hd, nk), head),
            pl.BlockSpec((1, hd, nk), head),
        ],
        out_shape=[
            jax.ShapeDtypeStruct((heads, hd, nq), bf16),
            jax.ShapeDtypeStruct((heads, hd, nk), bf16),
            jax.ShapeDtypeStruct((heads, hd, nk), bf16),
        ],
        compiler_params=pltpu.CompilerParams(vmem_limit_bytes=40 * 2**20),
        cost_estimate=pl.CostEstimate(
            flops=10 * heads * nq * nk * 128,
            bytes_accessed=8 * heads * hd * (nq + nk),
            transcendentals=heads * nq * nk,
        ),
        name="attend_bwd",
    )(length, q, k, v, g, log_total)


def norm_forward(state):
    center = state - jnp.mean(state, axis=0, keepdims=True)
    inverse = lax.rsqrt(jnp.mean(center * center, axis=0, keepdims=True) + norm_eps)
    return (center * inverse, inverse)


def norm_backward(grad_normed, normed, inverse):
    return inverse * (
        grad_normed
        - jnp.mean(grad_normed, axis=0, keepdims=True)
        - normed * jnp.mean(grad_normed * normed, axis=0, keepdims=True)
    )


def split_sum(partial_rows):
    other = swap(partial_rows[:, HALF:].astype(bf16), "col")
    return partial_rows[:, :HALF] + other.astype(f32)


def join_cols(own):
    return jnp.concatenate([own, swap(own, "col")], axis=1)


def through_in(own_w, other_w, rows):
    k = own_w.shape[0]
    return dot(own_w, rows[:k], 0, 0) + dot(other_w, rows[k:], 0, 0)


def reduce_weight(grads, order, row_index, dp_index):
    bits = lax.axis_size("dp").bit_length() - 1
    rows, n = grads.shape[1:]
    block = rows >> bits
    held = grads.reshape((2,) + (2,) * bits + (block, n))
    left = ["row"] + list(range(bits - 1, -1, -1))
    for step, name in enumerate(order):
        axis = left.index(name)
        if name == "row":
            keep = lax.index_in_dim(held, 0, axis, keepdims=False)
            send = lax.index_in_dim(held, 1, axis, keepdims=False)
            got = swap(send, "row")
        else:
            bit = (dp_index >> name) & 1
            first = lax.index_in_dim(held, 0, axis, keepdims=False)
            second = lax.index_in_dim(held, 1, axis, keepdims=False)
            keep = pick(first, second, bit)
            got = swap_dp(pick(second, first, bit), name)
        left.pop(axis)
        held = keep.astype(f32) + got.astype(f32)
        if step < len(order) - 1:
            held = held.astype(bf16)
    return held.reshape(block, n)


def local(
    latents,
    text,
    text_len,
    time_ids,
    time_table,
    shift_table,
    w_qkv,
    b_qv,
    w_out,
    b_out,
    w_cross_q,
    b_cross_q,
    w_cross_kv,
    b_cross_v,
    w_cross_out,
    b_cross_out,
    w_fc1,
    b_fc1,
    w_fc2,
    b_fc2,
    grad_out,
):
    quarter = latents.shape[1]
    half = 2 * quarter
    heads = half // HD
    n_dp = lax.axis_size("dp")
    bits = n_dp.bit_length() - 1
    d = lax.axis_index("dp")
    r = lax.axis_index("row")
    c = lax.axis_index("col")
    upper = d % 2
    pair = d // 2
    my_latent = pair * LPP + r

    def to_latent(values):
        turned = values.reshape(LPP, SEQ_DEV, quarter).transpose(0, 2, 1)
        mine, others = pick(turned[0], turned[1], r), pick(turned[1], turned[0], r)
        return jnp.stack([mine, swap(others, "row")])

    def all_features(halves):
        other = swap(halves, "col")
        both = jnp.stack([pick(halves, other, c), pick(other, halves, c)], axis=1)
        both = both.reshape(2 * half, SEQ_DEV)
        first, second = both[:, :HALF], both[:, HALF:]
        return jnp.concatenate([pick(first, second, c), pick(second, first, c)], axis=1)

    lat_half = to_latent(latents)
    lat_far = swap_dp(lat_half, 0)
    grad_half = to_latent(grad_out)
    w_qkv_o = swap(after(w_qkv, lat_far), "row")

    pair_times = lax.dynamic_slice_in_dim(time_ids, pair * LPP, LPP)
    one_hot = (
        pair_times[:, None] == jnp.arange(time_table.shape[0], dtype=jnp.int32)[None, :]
    ).astype(f32)
    modulation = shift_table[None] + jnp.einsum(
        "ln,nkf->lkf", one_hot, time_table, precision=lax.Precision.HIGHEST
    )
    feature_biases = jnp.stack([b_out, b_cross_out, b_fc2])
    wide = jnp.concatenate(
        [modulation, jnp.broadcast_to(feature_biases, (LPP, 3, quarter))], axis=1
    )
    col_biases = jnp.concatenate([b_qv.reshape(-1), b_cross_q, b_cross_v, b_fc1])
    sent = jnp.concatenate([pick(wide[1], wide[0], r).reshape(-1), col_biases])
    got = swap(sent, "row")
    wide_rows = jnp.stack([pick(wide[0], wide[1], r), got[: 9 * quarter].reshape(9, quarter)])
    wide_other = swap(wide_rows, "col")
    wide_all = jnp.stack(
        [pick(wide_rows, wide_other, c), pick(wide_other, wide_rows, c)], axis=1
    )
    vectors = wide_all.transpose(2, 0, 1, 3).reshape(9, 2 * half)
    shift_one, scale_one, gate_one, shift_two, scale_two, gate_two, bias_out, bias_co, bias_fc2 = (
        vectors[i][:, None] for i in range(9)
    )
    got_cols = got[9 * quarter :]

    def col_bias(start, width):
        return in_order(col_biases[start : start + width], got_cols[start : start + width], r, 0)

    bias_q = col_bias(0, quarter)[:, None]
    bias_v = col_bias(quarter, quarter)[:, None]
    bias_cq = col_bias(2 * quarter, quarter)[:, None]
    bias_cv = col_bias(3 * quarter, quarter)[:, None]
    bias_fc1 = col_bias(4 * quarter, b_fc1.shape[0])[:, None]

    text_own = text[0]
    text_row = in_order(text_own, swap(text_own, "col"), c, 1)
    kv_part = jnp.einsum("ti,iko->kot", text_row, w_cross_kv, preferred_element_type=f32)
    kv_total = kv_part + swap(kv_part.astype(bf16), "row").astype(f32)
    kv_total = jnp.concatenate(
        [kv_total[0].astype(bf16), (kv_total[1] + bias_cv).astype(bf16)]
    )
    kv_far = swap_dp(kv_total, 0)
    kv_mine = pick(kv_total, kv_far, r ^ upper).reshape(2, heads, HD, TXT)
    kv_mine = jnp.pad(kv_mine, ((0, 0), (0, 0), (0, 0), (0, TXT_PAD - TXT)))
    text_k, text_v = kv_mine[0], kv_mine[1]
    length = lax.dynamic_slice_in_dim(text_len, my_latent, 1)

    lat_all = jnp.concatenate([all_features(lat_half), all_features(lat_far)], axis=1).astype(f32)
    normed_all, inverse_all = norm_forward(lat_all)
    mod_all = (normed_all * (1.0 + scale_one) + shift_one).astype(bf16)
    normed_one, inverse_one = normed_all[:, :HALF], inverse_all[:, :HALF]
    mod_own = mod_all[:, :SEQ_DEV]
    w_q, w_k, w_v = (
        jnp.concatenate([w_qkv[:, i], w_qkv_o[:, i]], axis=0) for i in range(3)
    )
    keys = dot(w_k, mod_all, 0, 0).astype(bf16).reshape(heads, HD, -1)
    values = (dot(w_v, mod_all, 0, 0) + bias_v).astype(bf16).reshape(heads, HD, -1)
    queries = (dot(w_q, mod_own, 0, 0) + bias_q).astype(bf16).reshape(heads, HD, -1)
    w_out_o = swap(after(w_out, w_qkv_o), "row")
    w_cq_o = swap(after(w_cross_q, w_out_o), "row")
    w_co_o = swap(after(w_cross_out, w_cq_o), "row")
    w_fc1_o = swap(after(w_fc1, w_co_o), "row")
    w_fc2_o = swap(after(w_fc2, w_fc1_o), "row")
    attended, log_self = attend(queries, keys, values, length, False)
    attended = attended.reshape(half, -1)

    w_out_all = jnp.concatenate([w_out, w_out_o], axis=1)
    branch = split_sum(dot(w_out_all, attended, 0, 0)) + bias_out
    residual = lat_all[:, :HALF]
    after_self = residual + gate_one * branch
    cross_in = join_cols(after_self.astype(bf16))

    w_cq_all = jnp.concatenate([w_cross_q, w_cq_o], axis=0)
    cross_q = (dot(w_cq_all, cross_in, 0, 0) + bias_cq).astype(bf16).reshape(heads, HD, -1)
    crossed, log_cross = attend(cross_q, text_k, text_v, length, True)
    crossed = crossed.reshape(half, -1)
    w_co_all = jnp.concatenate([w_cross_out, w_co_o], axis=1)
    after_cross = after_self + split_sum(dot(w_co_all, crossed, 0, 0)) + bias_co

    normed_two, inverse_two = norm_forward(after_cross)
    mod_two = join_cols((normed_two * (1.0 + scale_two) + shift_two).astype(bf16))
    w_fc1_all = jnp.concatenate([w_fc1, w_fc1_o], axis=0)
    hidden = dot(w_fc1_all, mod_two, 0, 0) + bias_fc1
    activated = jax.nn.gelu(hidden, approximate=True).astype(bf16)

    grad_all = all_features(grad_half).astype(f32)
    grad_mlp = (gate_two * grad_all).astype(bf16)
    w_fc2_all = jnp.concatenate([w_fc2, w_fc2_o], axis=1)
    grad_activated = dot(w_fc2_all, grad_mlp, 1, 0)
    grad_hidden = jax.vjp(partial(jax.nn.gelu, approximate=True), hidden)[1](grad_activated)[0]
    grad_b_fc1 = jnp.sum(grad_hidden, axis=1)
    grad_hidden = grad_hidden.astype(bf16)

    def weight_grad_in(inputs, grads):
        return dot(inputs, grads, 1, 1).astype(bf16).reshape(2, -1, grads.shape[0])

    def weight_grad_out(inputs, grads):
        n = grads.shape[0] // 2
        return jnp.stack([dot(inputs, g, 1, 1).astype(bf16) for g in (grads[:n], grads[n:])])

    dp_bits = list(range(bits))
    order_x = ["row"] + dp_bits
    order_y = [0, "row"] + dp_bits[1:]
    order_z = [1, "row", 0] + dp_bits[2:]
    summed_fc2 = reduce_weight(weight_grad_out(activated, grad_mlp), order_x, r, d)
    summed_fc1 = reduce_weight(weight_grad_in(mod_two, grad_hidden), order_y, r, d)

    grad_mod_two = split_sum(dot(w_fc1_all, grad_hidden, 1, 0))
    grad_own = grad_all[:, :HALF]
    grad_after_cross = grad_own + norm_backward(
        grad_mod_two * (1.0 + scale_two), normed_two, inverse_two
    )
    grad_cross = join_cols(grad_after_cross.astype(bf16))

    mlp_out = split_sum(dot(w_fc2_all, activated, 0, 0)) + bias_fc2
    result = (after_cross + gate_two * mlp_out).astype(bf16)

    grad_crossed = dot(w_co_all, grad_cross, 1, 0).astype(bf16).reshape(heads, HD, -1)
    summed_co = reduce_weight(weight_grad_out(crossed, grad_cross), order_z, r, d)
    grad_cq, grad_tk, grad_tv = attend_grad(
        cross_q, text_k, text_v, grad_crossed, log_cross, length, True
    )
    grad_cq = grad_cq.reshape(half, -1)
    summed_cq = reduce_weight(weight_grad_in(cross_in, grad_cq), order_z, r, d)
    grad_b_cq = jnp.sum(grad_cq.astype(f32), axis=1)
    grad_after_self = grad_after_cross + split_sum(dot(w_cq_all, grad_cq, 1, 0))
    grad_branch = join_cols((gate_one * grad_after_self).astype(bf16))

    grad_kv = jnp.stack([grad_tk, grad_tv])[..., :TXT].reshape(2, half, TXT)
    grad_kv = grad_kv.astype(f32) + swap_dp(grad_kv, 0).astype(f32)
    grad_b_cv = jnp.sum(grad_kv[1], axis=1)
    grad_kv_latent = grad_kv.astype(bf16)
    grad_kv_other = swap(grad_kv_latent, "row")
    grad_kv_own = pick(grad_kv_latent, grad_kv_other, r ^ upper)
    grad_text_part = jnp.einsum(
        "kot,iko->ti", grad_kv_own, w_cross_kv, preferred_element_type=f32
    )
    text_quarter = text.shape[2]
    keep_text = pick(grad_text_part[:, :text_quarter], grad_text_part[:, text_quarter:], c)
    send_text = pick(grad_text_part[:, text_quarter:], grad_text_part[:, :text_quarter], c)
    grad_text = (keep_text + swap(send_text.astype(bf16), "col").astype(f32))[None]
    blocks = text_row.reshape((TXT,) + (2,) * bits + (-1,))
    held = blocks[None]
    kv_held = grad_kv_own[None]
    for bit in range(bits):
        axis = held.ndim - 2
        first = lax.index_in_dim(held, 0, axis, keepdims=False)
        second = lax.index_in_dim(held, 1, axis, keepdims=False)
        mine = (d >> bit) & 1
        got_text = swap_dp(pick(second, first, mine), bit)
        held = jnp.concatenate([pick(first, second, mine), got_text], axis=0)
        kv_held = jnp.concatenate([kv_held, swap_dp(kv_held, bit)], axis=0)
    summed_ckv = jnp.einsum("lti,lkot->iko", held, kv_held, preferred_element_type=f32)

    grad_attended = dot(w_out_all, grad_branch, 1, 0).astype(bf16).reshape(heads, HD, -1)
    summed_out = reduce_weight(weight_grad_out(attended, grad_branch), order_z, r, d)
    grad_q, grad_k, grad_v = attend_grad(
        queries, keys, values, grad_attended, log_self, length, False
    )
    grad_q, grad_k, grad_v = (g.reshape(half, -1) for g in (grad_q, grad_k, grad_v))
    summed_k = reduce_weight(weight_grad_in(mod_all, grad_k), order_x, r, d)
    summed_v = reduce_weight(weight_grad_in(mod_all, grad_v), order_y, r, d)
    summed_q = reduce_weight(weight_grad_in(mod_own, grad_q), order_z, r, d)
    summed_qkv = jnp.stack([summed_q, summed_k, summed_v], axis=1)
    grad_b_q = jnp.sum(grad_q.astype(f32), axis=1)
    grad_b_v = jnp.sum(grad_v.astype(f32), axis=1)
    grad_mod_kv = dot(w_k, grad_k, 1, 0) + dot(w_v, grad_v, 1, 0)
    far_part = swap_dp(split_sum(grad_mod_kv[:, SEQ_DEV:]).astype(bf16), 0)
    near_part = split_sum(grad_mod_kv[:, :SEQ_DEV] + dot(w_q, grad_q, 1, 0))
    grad_mod_one = near_part + far_part.astype(f32)
    grad_latents = grad_after_self + norm_backward(
        grad_mod_one * (1.0 + scale_one), normed_one, inverse_one
    )

    def to_features(own):
        blocks = own.reshape(2, 2, quarter, HALF)
        keep = pick(blocks[:, 0], blocks[:, 1], c)
        got = swap(pick(blocks[:, 1], blocks[:, 0], c), "col")
        tokens = in_order(keep, got, c, 2)
        other = swap(tokens[1], "row")
        return in_order(tokens[0].T, other.T, r, 0)

    output = to_features(result)
    grad_latents = to_features(grad_latents.astype(bf16)).astype(f32)

    grad_vectors = jnp.stack(
        [
            jnp.sum(grad_mod_one, axis=1),
            jnp.sum(grad_mod_one * normed_one, axis=1),
            jnp.sum(grad_after_self * branch, axis=1),
            jnp.sum(grad_mod_two, axis=1),
            jnp.sum(grad_mod_two * normed_two, axis=1),
            jnp.sum(grad_own * mlp_out, axis=1),
            gate_one[:, 0] * jnp.sum(grad_after_self, axis=1),
            jnp.sum(grad_after_cross, axis=1),
            gate_two[:, 0] * jnp.sum(grad_own, axis=1),
        ]
    ).reshape(9, 2, 2, quarter)
    keep = pick(grad_vectors[:, :, 0], grad_vectors[:, :, 1], c)
    keep = keep + swap(pick(grad_vectors[:, :, 1], grad_vectors[:, :, 0], c), "col")
    col_grads = jnp.concatenate(
        [
            g.reshape(2, -1)
            for g in (grad_b_q, grad_b_v, grad_b_cq, grad_b_cv, grad_b_fc1)
        ],
        axis=1,
    )
    pair_once = jnp.concatenate(
        [
            jnp.ones((3 * quarter,), f32),
            jnp.full((quarter,), 0.5, f32),
            jnp.ones((col_grads.shape[1] - 4 * quarter,), f32),
        ]
    )
    col_grads = col_grads * pair_once
    mine_cols = pick(col_grads[0], col_grads[1], r)
    sent = jnp.concatenate([keep[:, 1].reshape(-1), pick(col_grads[1], col_grads[0], r)])
    got = swap(sent, "row")
    got_wide = got[: 9 * quarter].reshape(9, quarter)
    own_wide = keep[:, 0]
    latent_wide = jnp.stack([pick(own_wide, got_wide, r), pick(got_wide, own_wide, r)])
    mine_cols = mine_cols + got[9 * quarter :]
    table_part = jnp.einsum(
        "ln,lkf->nkf", one_hot, latent_wide[:, :6], precision=lax.Precision.HIGHEST
    )
    ntab = time_table.shape[0]
    flat = jnp.concatenate(
        [table_part.reshape(-1), (own_wide + got_wide).reshape(-1), mine_cols]
    )
    for bit in range(bits):
        flat = flat + swap_dp(flat, bit)
    n_table = ntab * 6 * quarter
    grad_time_table = flat[:n_table].reshape(ntab, 6, quarter)
    rest = flat[n_table:]
    wide_sums = rest[: 9 * quarter].reshape(9, quarter)
    grad_shift_table = wide_sums[:6]
    cols = rest[9 * quarter :]
    grad_b_qv = cols[: 2 * quarter].reshape(2, quarter)
    return (
        output,
        grad_latents,
        grad_text,
        grad_time_table,
        grad_shift_table,
        summed_qkv,
        grad_b_qv,
        summed_out,
        wide_sums[6],
        summed_cq,
        cols[2 * quarter : 3 * quarter],
        summed_ckv,
        cols[3 * quarter : 4 * quarter],
        summed_co,
        wide_sums[7],
        summed_fc1,
        cols[4 * quarter :],
        summed_fc2,
        wide_sums[8],
    )


def solution(mesh):
    return jax.shard_map(
        local,
        mesh=mesh,
        in_specs=(
            P("dp", ("row", "col")),
            P("dp", None, ("row", "col")),
            P(),
            P(),
            P(None, None, ("row", "col")),
            P(None, ("row", "col")),
            P("row", None, "col"),
            P(None, ("col", "row")),
            P("col", "row"),
            P(("row", "col")),
            P("row", "col"),
            P(("col", "row")),
            P("row", None, "col"),
            P(("col", "row")),
            P("col", "row"),
            P(("row", "col")),
            P("row", "col"),
            P(("col", "row")),
            P("col", "row"),
            P(("row", "col")),
            P("dp", ("row", "col")),
        ),
        out_specs=(
            P("dp", ("row", "col")),
            P("dp", ("row", "col")),
            P("dp", None, ("row", "col")),
            P(None, None, ("row", "col")),
            P(None, ("row", "col")),
            P(("row", "dp"), None, "col"),
            P(None, ("col", "row")),
            P(("col", "dp"), "row"),
            P(("row", "col")),
            P(("row", "dp"), "col"),
            P(("col", "row")),
            P(("row", "dp"), None, "col"),
            P(("col", "row")),
            P(("col", "dp"), "row"),
            P(("row", "col")),
            P(("row", "dp"), "col"),
            P(("col", "row")),
            P(("col", "dp"), "row"),
            P(("row", "col")),
        ),
        check_vma=False,
    )
```

```python
from functools import partial

import jax
import jax.numpy as jnp
from jax import lax
from jax.experimental import pallas as pl
from jax.experimental.pallas import tpu as pltpu
from jax.sharding import PartitionSpec as P

HD = 72
TXT = 120
TXT_PAD = 128
SEQ_DEV = 512
LPP = 2
HALF = 256

norm_eps = 1e-06
masked_score = -1000000000.0
f32 = jnp.float32
bf16 = jnp.bfloat16
SMALL_COST = pl.CostEstimate(flops=1, bytes_accessed=1, transcendentals=0)


def swap(value, axis):
    return lax.ppermute(value, axis, [(0, 1), (1, 0)])


def swap_dp(value, bit):
    return lax.ppermute(value, "dp", [(i, i ^ (1 << bit)) for i in range(lax.axis_size("dp"))])


def pick(pair_first, pair_second, index):
    return jnp.where(index == 0, pair_first, pair_second)


def in_order(mine, other, index, axis):
    return jnp.concatenate([pick(mine, other, index), pick(other, mine, index)], axis=axis)


def after(value, *earlier):
    return lax.optimization_barrier((value, *earlier))[0]


def dot(left, right, left_dim, right_dim):
    return lax.dot_general(
        left, right, (((left_dim,), (right_dim,)), ((), ())), preferred_element_type=f32
    )


def scores_of(masked, length_ref, q, k):
    scores = dot(k, q, 0, 0) * (HD ** (-0.5))
    if masked:
        place = lax.broadcasted_iota(jnp.int32, scores.shape, 0)
        scores = jnp.where(place < length_ref[0], scores, masked_score)
    return scores


def attend_kernel(masked, length_ref, q_ref, k_ref, v_ref, o_ref, log_ref):
    scores = scores_of(masked, length_ref, q_ref[0], k_ref[0])
    largest = jnp.max(scores, axis=0, keepdims=True)
    raised = jnp.exp(scores - largest)
    total = jnp.sum(raised, axis=0, keepdims=True)
    mixture = dot(v_ref[0], raised.astype(bf16), 1, 0)
    o_ref[0] = (mixture / total).astype(bf16)
    log_ref[0] = largest + jnp.log(total)


def attend(q, k, v, length, masked):
    heads, hd, nq = q.shape
    nk = k.shape[2]
    head = lambda h: (h, 0, 0)
    return pl.pallas_call(
        partial(attend_kernel, masked),
        grid=(heads,),
        in_specs=[
            pl.BlockSpec(memory_space=pltpu.SMEM),
            pl.BlockSpec((1, hd, nq), head),
            pl.BlockSpec((1, hd, nk), head),
            pl.BlockSpec((1, hd, nk), head),
        ],
        out_specs=[pl.BlockSpec((1, hd, nq), head), pl.BlockSpec((1, 1, nq), head)],
        out_shape=[
            jax.ShapeDtypeStruct((heads, hd, nq), bf16),
            jax.ShapeDtypeStruct((heads, 1, nq), f32),
        ],
        compiler_params=pltpu.CompilerParams(vmem_limit_bytes=32 * 2**20),
        cost_estimate=SMALL_COST,
        name="attend_fwd",
    )(length, q, k, v)


def attend_grad_kernel(
    masked, length_ref, q_ref, k_ref, v_ref, g_ref, log_ref, dq_ref, dk_ref, dv_ref
):
    q, k, v, g = q_ref[0], k_ref[0], v_ref[0], g_ref[0]
    weights = jnp.exp(scores_of(masked, length_ref, q, k) - log_ref[0])
    grad_weights = dot(v, g, 0, 0)
    crossed = jnp.sum(grad_weights * weights, axis=0, keepdims=True)
    grad_scores = (weights * (grad_weights - crossed)).astype(bf16)
    dq_ref[0] = (dot(k, grad_scores, 1, 0) * (HD ** (-0.5))).astype(bf16)
    dk_ref[0] = (dot(q, grad_scores, 1, 1) * (HD ** (-0.5))).astype(bf16)
    dv_ref[0] = dot(g, weights.astype(bf16), 1, 1).astype(bf16)


def attend_grad(q, k, v, g, log_total, length, masked):
    heads, hd, nq = q.shape
    nk = k.shape[2]
    head = lambda h: (h, 0, 0)
    queries, keys = pl.BlockSpec((1, hd, nq), head), pl.BlockSpec((1, hd, nk), head)
    return pl.pallas_call(
        partial(attend_grad_kernel, masked),
        grid=(heads,),
        in_specs=[
            pl.BlockSpec(memory_space=pltpu.SMEM),
            queries,
            keys,
            keys,
            queries,
            pl.BlockSpec((1, 1, nq), head),
        ],
        out_specs=[queries, keys, keys],
        out_shape=[
            jax.ShapeDtypeStruct((heads, hd, nq), bf16),
            jax.ShapeDtypeStruct((heads, hd, nk), bf16),
            jax.ShapeDtypeStruct((heads, hd, nk), bf16),
        ],
        compiler_params=pltpu.CompilerParams(vmem_limit_bytes=40 * 2**20),
        cost_estimate=SMALL_COST,
        name="attend_bwd",
    )(length, q, k, v, g, log_total)


def assemble_kernel(kind, core_ref, mine_ref, other_ref, vectors_ref, *outs):
    quarter = mine_ref.shape[1]
    held = outs[-1]
    core = core_ref[0]
    for row in range(2):
        mine = pl.multiple_of((2 * row + core) * quarter, 16)
        other = pl.multiple_of((2 * row + 1 - core) * quarter, 16)
        held[pl.ds(mine, quarter), :] = mine_ref[row].astype(f32)
        held[pl.ds(other, quarter), :] = other_ref[row].astype(f32)
    state = held[...]
    if kind == "gate":
        outs[0][...] = state.astype(bf16)
        outs[1][...] = (state * vectors_ref[:, 5:6]).astype(bf16)
    else:
        mean = jnp.mean(state, axis=0, keepdims=True)
        center = state - mean
        inverse = lax.rsqrt(jnp.mean(center * center, axis=0, keepdims=True) + norm_eps)
        outs[0][...] = state.astype(bf16)
        scale, shift = 1.0 + vectors_ref[:, 1:2], vectors_ref[:, 0:1]
        outs[1][...] = (center * inverse * scale + shift).astype(bf16)
        outs[2][...] = mean
        outs[3][...] = inverse


def assemble(kind, mine, other, core, vectors):
    _, quarter, tokens = mine.shape
    features = 4 * quarter
    place = lambda t, core_ref: (0, 0, t - t % 2 + (t + core_ref[0]) % 2)
    columns = pl.BlockSpec(vectors.shape, lambda t, core_ref: (0, 0))
    block = pl.BlockSpec((features, HALF), lambda t, core_ref: (0, t))
    line = pl.BlockSpec((1, HALF), lambda t, core_ref: (0, t))
    outs, shapes = [block, block], [jax.ShapeDtypeStruct((features, tokens), bf16)] * 2
    if kind == "norm":
        outs, shapes = outs + [line] * 2, shapes + [jax.ShapeDtypeStruct((1, tokens), f32)] * 2
    return pl.pallas_call(
        partial(assemble_kernel, kind),
        grid_spec=pltpu.PrefetchScalarGridSpec(
            num_scalar_prefetch=1,
            grid=(tokens // HALF,),
            in_specs=[pl.BlockSpec((2, quarter, HALF), place)] * 2 + [columns],
            out_specs=outs,
            scratch_shapes=[pltpu.VMEM((features, HALF), f32)],
        ),
        out_shape=shapes,
        compiler_params=pltpu.CompilerParams(vmem_limit_bytes=32 * 2**20),
        cost_estimate=SMALL_COST,
        name="assemble_" + kind,
    )(core, mine, other, vectors)


class Weight:
    def __init__(self, pieces, places):
        self.arrays = [array for array, _ in pieces]
        self.leads = [lead for _, lead in pieces]
        self.rows = [array.shape[-2] for array in self.arrays]
        self.n = self.arrays[0].shape[-1]
        self.places = jnp.stack([jnp.asarray(place, jnp.int32) for place in places])

    def specs(self, cols, column):
        def spec(rows, lead):
            if lead is None:
                return pl.BlockSpec((rows, cols), lambda *grid: (0, column(*grid)))
            return pl.BlockSpec((None, rows, cols), lambda *grid: (lead, 0, column(*grid)))

        return [spec(rows, lead) for rows, lead in zip(self.rows, self.leads)]


def place_of(places_ref, index):
    return pl.multiple_of(places_ref[index], 16)


def gelu_parts(v):
    inner = 0.7978845608028654 * (v + 0.044715 * (v * v * v))
    bent = jnp.tanh(inner)
    slope = 0.7978845608028654 * (1.0 + 3 * 0.044715 * (v * v))
    return 0.5 * v * (1.0 + bent), 0.5 * (1.0 + bent) + 0.5 * v * (1.0 - bent * bent) * slope


def rows_in_kernel(count, kind, lane, places_ref, x_ref, *refs):
    pieces, rest = refs[:count], refs[count:]
    total = None
    for index, piece in enumerate(pieces):
        rows = x_ref[pl.ds(place_of(places_ref, index), piece.shape[0]), :]
        part = dot(piece[...], rows, 0, 0)
        total = part if total is None else total + part
    if kind == "plain":
        rest[0][...] = total.astype(bf16)
    elif kind == "bias":
        rest[1][...] = (total + rest[0][:, lane : lane + 1]).astype(bf16)
    elif kind == "gelu":
        value, slope = gelu_parts(total + rest[0][...])
        rest[1][...] = value.astype(bf16)
        rest[2][...] = slope.astype(bf16)
    elif kind == "slope":
        grad = total * rest[0][...].astype(f32)
        rest[1][...] = grad.astype(bf16)
        rest[2][...] = jnp.sum(grad, axis=1, keepdims=True)


def rows_in(weight, x, kind="plain", operand=None, lane=0):
    k, tokens = x.shape
    n = weight.n
    cols = 768 if n % 768 == 0 else n
    wide = min(tokens, 512)
    out_block = pl.BlockSpec((cols, wide), lambda i, t: (i, t))
    column = pl.BlockSpec((cols, 1), lambda i, t: (i, 0))
    out = jax.ShapeDtypeStruct((n, tokens), bf16)
    lanes = pl.BlockSpec((cols, operand.shape[1]), lambda i, t: (i, 0)) if kind == "bias" else None
    extra = {"plain": [], "bias": [lanes], "gelu": [column], "slope": [out_block]}[kind]
    specs, shapes = [out_block], [out]
    if kind == "gelu":
        specs, shapes = [out_block] * 2, [out] * 2
    if kind == "slope":
        specs, shapes = [out_block, column], [out, jax.ShapeDtypeStruct((n, 1), f32)]
    result = pl.pallas_call(
        partial(rows_in_kernel, len(weight.arrays), kind, lane),
        grid=(n // cols, tokens // wide),
        in_specs=[
            pl.BlockSpec(memory_space=pltpu.SMEM),
            pl.BlockSpec((k, wide), lambda i, t: (0, t)),
        ]
        + weight.specs(cols, lambda i, t: i)
        + extra,
        out_specs=specs,
        out_shape=shapes,
        compiler_params=pltpu.CompilerParams(vmem_limit_bytes=48 * 2**20),
        cost_estimate=SMALL_COST,
        name="rows_in_" + kind,
    )(weight.places, x, *weight.arrays, *([] if operand is None else [operand]))
    return result[0] if len(result) == 1 else result


def rows_out_kernel(counts, steps, *refs):
    sides = len(counts)
    places, ys = refs[:sides], refs[sides : 2 * sides]
    pieces, (keep_ref, send_ref) = refs[2 * sides : -2], refs[-2:]
    step = pl.program_id(0)

    def rows_of(side, index, piece):
        return pl.ds(place_of(places[side], index), piece.shape[0])

    def write(target, active):
        start = 0
        for side in range(sides):
            if side in active:
                for index, piece in enumerate(pieces[start : start + counts[side]]):
                    rows = rows_of(side, index, piece)
                    part = dot(piece[...], ys[side][...], 1, 0)
                    if side != active[0]:
                        part = part + target[rows, :].astype(f32)
                    target[rows, :] = part.astype(target.dtype)
            start += counts[side]

    for number in range(max(steps)):
        active = [side for side in range(sides) if number < steps[side]]

        @pl.when(step == number)
        def _():
            write(keep_ref if number % 2 == 0 else send_ref, active)


def rows_out(pairs):
    k = 2 * pairs[0][0].rows[0]
    steps = [y.shape[1] // HALF for _, y in pairs]
    most = max(steps)

    def y_spec(y, count):
        return pl.BlockSpec((y.shape[0], HALF), lambda t: (0, jnp.minimum(t, count - 1)))

    in_specs = [pl.BlockSpec(memory_space=pltpu.SMEM) for _ in pairs]
    in_specs += [y_spec(y, count) for (_, y), count in zip(pairs, steps)]
    operands = [w.places for w, _ in pairs] + [y for _, y in pairs]
    for w, _ in pairs:
        in_specs += w.specs(w.n, lambda t: 0)
        operands += w.arrays
    width = most // 2 * HALF
    out_block = pl.BlockSpec((k, HALF), lambda t: (0, t // 2))
    return pl.pallas_call(
        partial(rows_out_kernel, [len(w.arrays) for w, _ in pairs], steps),
        grid=(most,),
        in_specs=in_specs,
        out_specs=[out_block, out_block],
        out_shape=[jax.ShapeDtypeStruct((k, width), f32), jax.ShapeDtypeStruct((k, width), bf16)],
        compiler_params=pltpu.CompilerParams(vmem_limit_bytes=48 * 2**20),
        cost_estimate=SMALL_COST,
        name="rows_out",
    )(*operands)


def weight_grad_kernel(inputs_ref, grads_ref, out_ref):
    out_ref[0] = dot(inputs_ref[...], grads_ref[0], 1, 1).astype(bf16)


def weight_grad(inputs, grads, first=0, groups=None):
    k, tokens = inputs.shape
    total, n, _ = grads.shape
    groups = total if groups is None else groups
    rows = 384 if k % 384 == 0 else 288
    return pl.pallas_call(
        weight_grad_kernel,
        grid=(groups, k // rows),
        in_specs=[
            pl.BlockSpec((rows, tokens), lambda g, i: (i, 0)),
            pl.BlockSpec((1, n, tokens), lambda g, i: (first + g, 0, 0)),
        ],
        out_specs=pl.BlockSpec((1, rows, n), lambda g, i: (g, i, 0)),
        out_shape=jax.ShapeDtypeStruct((groups, k, n), bf16),
        compiler_params=pltpu.CompilerParams(vmem_limit_bytes=40 * 2**20),
        cost_estimate=SMALL_COST,
        name="weight_grad",
    )(inputs, grads)


def norm_forward(state):
    center = state - jnp.mean(state, axis=0, keepdims=True)
    inverse = lax.rsqrt(jnp.mean(center * center, axis=0, keepdims=True) + norm_eps)
    return (center * inverse, inverse)


def norm_backward(grad_normed, normed, inverse):
    return inverse * (
        grad_normed
        - jnp.mean(grad_normed, axis=0, keepdims=True)
        - normed * jnp.mean(grad_normed * normed, axis=0, keepdims=True)
    )


def split_sum(pairs):
    keep, send = rows_out(pairs)
    return keep + swap(send, "col").astype(f32)


def join_cols(own):
    return jnp.concatenate([own, swap(own, "col")], axis=1)


def reduce_pieces(held, order, dp_index):
    bits = lax.axis_size("dp").bit_length() - 1
    left = ["row"] + list(range(bits - 1, -1, -1))
    for step, name in enumerate(order):
        axis = left.index(name)
        if name == "row":
            keep = lax.index_in_dim(held, 0, axis, keepdims=False)
            send = lax.index_in_dim(held, 1, axis, keepdims=False)
        else:
            bit = (dp_index >> name) & 1
            keep = lax.dynamic_index_in_dim(held, bit, axis, keepdims=False)
            send = lax.dynamic_index_in_dim(held, 1 - bit, axis, keepdims=False)
        got = yield (name, send)
        left.pop(axis)
        held = keep.astype(f32) + got.astype(f32)
        if step < len(order) - 1:
            held = held.astype(bf16)
    return held


class Task:
    def __init__(self, steps):
        self.steps, self.done, self.result, self.half = steps, False, None, None


class Links:
    def __init__(self):
        self.free, self.events, self.waits = {}, [], []
        self.last, self.now, self.count, self.halves = None, 0.0, 0, []

    def push(self, time, task, got, tie):
        self.count += 1
        self.events.append((time, self.count, task, got, tie))

    def spawn(self, steps):
        task = Task(steps)
        self.push(self.now, task, None, False)
        return task

    def ask(self, task, request):
        kind = request[0]
        if kind == "wait":
            self.waits.append((task, request[1]))
            return
        if kind == "half":
            self.halves.append((task, request[1]))
            return
        if kind == "set":
            task.half = request[1]
            self.push(self.now, task, None, False)
            return
        if kind == "compute":
            end = max(self.now, self.free.get("compute", 0.0)) + request[2]
            self.free["compute"] = end
            self.push(end, task, request[1], True)
            return
        value = request[1]
        link = {"row": "x", 0: "y"}.get(kind, "z")
        hops = 2 ** max(kind - 1, 0) if isinstance(kind, int) else 1
        end = max(self.now, self.free.get(link, 0.0)) + 2.0
        end += hops * value.size * value.dtype.itemsize / 46e3
        self.free[link] = end
        got = swap_dp(value, kind) if isinstance(kind, int) else swap(value, kind)
        self.push(end, task, got, True)

    def run(self):
        while self.events:
            event = min(self.events, key=lambda item: item[:2])
            self.events.remove(event)
            self.now, _, task, got, tie = event
            if tie:
                if self.last is not None:
                    got = after(got, self.last)
                self.last = got
            try:
                self.ask(task, task.steps.send(got))
            except StopIteration as stop:
                task.done, task.result = True, stop.value
            still = []
            for waiting, others in self.waits:
                if all(other.done for other in others):
                    self.push(self.now, waiting, [other.result for other in others], False)
                else:
                    still.append((waiting, others))
            self.waits = still
            for waiting, other in [pair for pair in self.halves if pair[1].half is not None]:
                self.halves.remove((waiting, other))
                self.push(self.now, waiting, None, False)


def local(
    latents,
    text,
    text_len,
    time_ids,
    time_table,
    shift_table,
    w_qkv,
    b_qv,
    w_out,
    b_out,
    w_cross_q,
    b_cross_q,
    w_cross_kv,
    b_cross_v,
    w_cross_out,
    b_cross_out,
    w_fc1,
    b_fc1,
    w_fc2,
    b_fc2,
    grad_out,
):
    quarter = latents.shape[1]
    half = 2 * quarter
    heads = half // HD
    n_dp = lax.axis_size("dp")
    bits = n_dp.bit_length() - 1
    d = lax.axis_index("dp")
    r = lax.axis_index("row")
    c = lax.axis_index("col")
    upper = d % 2
    pair = d // 2
    my_latent = pair * LPP + r

    def own_and_sent(values):
        turned = values.T
        return tuple(
            lax.dynamic_slice_in_dim(turned, place * SEQ_DEV, SEQ_DEV, 1) for place in (r, 1 - r)
        )

    links = Links()
    core = c[None].astype(jnp.int32)

    def fetch(blocks, first, bit, behind, *choices):
        w, (rows, n) = len(choices), blocks.shape[1:]
        if behind is not None:
            yield ("half", behind)
            blocks = after(blocks, behind.half)
        mine = (d >> bit) & 1
        half_rows = rows // 2
        got = yield (
            "row",
            lax.dynamic_slice(blocks, (first, mine * half_rows, 0), (w, half_rows, n)),
        )
        yield ("set", got)
        relayed = yield (bit, got)
        more = [(got, rows + half_rows * mine), (relayed, rows + half_rows * (1 - mine))]
        return [
            Weight([own] + [(array, i) for array, _ in more], [0] + [place for _, place in more])
            for i, own in enumerate(choices)
        ]

    def near_task(values):
        own, sent = own_and_sent(values)
        return jnp.stack([own, (yield ("row", sent))])

    def latents_in_task():
        near = yield from near_task(latents)
        far = yield (0, near)
        both = jnp.concatenate([near, far], axis=-1)
        return both, swap(both, "col")

    def grad_out_task():
        near = yield from near_task(grad_out)
        return near, swap(near, "col")

    def vectors_in_task():
        pair_times = lax.dynamic_slice_in_dim(time_ids, pair * LPP, LPP)
        one_hot = hot_of(pair_times)
        modulation = shift_table[None] + jnp.einsum(
            "ln,nkf->lkf", one_hot, time_table, precision=lax.Precision.HIGHEST
        )
        feature_biases = jnp.stack([b_out, b_cross_out, b_fc2])
        wide = jnp.concatenate(
            [modulation, jnp.broadcast_to(feature_biases, (LPP, 3, quarter))], axis=1
        )
        col_biases = jnp.concatenate([b_qv.reshape(-1), b_cross_q, b_cross_v, b_fc1])
        got = yield (
            "row",
            jnp.concatenate([pick(wide[1], wide[0], r).reshape(-1), col_biases]),
        )
        wide_rows = jnp.stack(
            [pick(wide[0], wide[1], r), got[: 9 * quarter].reshape(9, quarter)]
        )
        wide_other = swap(wide_rows, "col")
        wide_all = jnp.stack(
            [pick(wide_rows, wide_other, c), pick(wide_other, wide_rows, c)], axis=1
        )
        vectors = wide_all.transpose(0, 1, 3, 2).reshape(2 * half, 9)
        got_cols = got[9 * quarter :]
        four, four_got = (v[: 4 * quarter].reshape(4, quarter) for v in (col_biases, got_cols))
        fc1 = in_order(col_biases[4 * quarter :], got_cols[4 * quarter :], r, 0)[:, None]
        return vectors, in_order(four, four_got, r, 1).T, fc1

    def spread_task():
        yield ("wait", [fetch_three])
        return (yield ("compute", text_all, 0.0))

    def captions_in_task():
        ((_, cols, _),) = yield ("wait", [vectors_in])
        kv_part = jnp.einsum("ti,iko->kot", text_row, w_cross_kv, preferred_element_type=f32)
        far = yield ("row", kv_part.astype(bf16))
        kv_total = kv_part + far.astype(f32)
        kv_total = jnp.concatenate(
            [kv_total[0].astype(bf16), (kv_total[1] + cols[:, 3:]).astype(bf16)]
        )
        kv_far = yield (0, kv_total)
        kv_mine = pick(kv_total, kv_far, r ^ upper).reshape(2, heads, HD, TXT)
        kv_mine = jnp.pad(kv_mine, ((0, 0), (0, 0), (0, 0), (0, TXT_PAD - TXT)))
        return kv_mine[0], kv_mine[1]

    dp_bits = list(range(bits))
    order_x = ["row"] + dp_bits
    order_y = [0, "row"] + dp_bits[1:]
    order_z = [1, "row", 0] + dp_bits[2:]

    def by_block(grads, n):
        return grads.reshape((2,) + (2,) * bits + (-1, n))

    def reduce(grads, order):
        return links.spawn(reduce_pieces(grads, order, d))

    def to_features(own):
        blocks = own.reshape(2, 2, quarter, HALF)
        keep = lax.dynamic_index_in_dim(blocks, c, 1, keepdims=False)
        got = swap(lax.dynamic_index_in_dim(blocks, 1 - c, 1, keepdims=False), "col")
        tokens = in_order(keep, got, c, 2)
        other = yield ("row", tokens[1])
        return in_order(tokens[0], other, r, 1).T

    def main_task():
        ((lat_both, lat_other), (vectors, biases, bias_fc1)) = yield (
            "wait",
            [latents_in, vectors_in],
        )
        shift_one, scale_one, gate_one, shift_two, scale_two, gate_two = (
            vectors[:, i : i + 1] for i in range(6)
        )
        bias_out, bias_co, bias_fc2 = (vectors[:, i : i + 1] for i in range(6, 9))
        lat_all, mod_all, mean_all, inverse_all = assemble(
            "norm", lat_both, lat_other, core, vectors
        )
        mod_all = yield ("compute", mod_all, 6.0)
        mod_own = mod_all[:, :SEQ_DEV]
        ((weight_k, weight_v),) = yield ("wait", [fetch_kv])
        keys = rows_in(weight_k, mod_all).reshape(heads, HD, -1)
        values = rows_in(weight_v, mod_all, "bias", biases, 1).reshape(heads, HD, -1)
        values = yield ("compute", values, 8.0)
        ((weight_q,),) = yield ("wait", [fetch_q])
        queries = rows_in(weight_q, mod_own, "bias", biases, 0).reshape(heads, HD, -1)
        attended, log_self = attend(queries, keys, values, length, False)
        attended = yield ("compute", attended, 13.0)
        attended = attended.reshape(half, -1)
        ((weight_out, weight_cq, weight_co),) = yield ("wait", [fetch_three])
        branch = split_sum([(weight_out, attended)]) + bias_out
        residual = lat_all[:, :HALF].astype(f32)
        after_self = residual + gate_one * branch
        cross_in = join_cols(after_self.astype(bf16))
        cross_in = yield ("compute", cross_in, 12.0)

        ((text_k, text_v),) = yield ("wait", [captions_in])
        cross_q = rows_in(weight_cq, cross_in, "bias", biases, 2).reshape(heads, HD, -1)
        crossed, log_cross = attend(cross_q, text_k, text_v, length, True)
        crossed = yield ("compute", crossed, 8.0)
        crossed = crossed.reshape(half, -1)
        after_cross = after_self + split_sum([(weight_co, crossed)]) + bias_co

        normed_two, inverse_two = norm_forward(after_cross)
        mod_two = join_cols((normed_two * (1.0 + scale_two) + shift_two).astype(bf16))
        mod_two = yield ("compute", mod_two, 15.0)
        ((weight_fc1,),) = yield ("wait", [fetch_fc1])
        activated, slope = rows_in(weight_fc1, mod_two, "gelu", bias_fc1)
        activated = yield ("compute", activated, 10.0)

        ((grad_near, grad_other),) = yield ("wait", [grad_in])
        grad_all, grad_mlp = assemble("gate", grad_near, grad_other, core, vectors)
        grad_w_fc2 = by_block(weight_grad(activated, grad_mlp.reshape(2, half, -1)), half)
        grad_w_fc2 = yield ("compute", grad_w_fc2, 9.0)
        sum_fc2 = reduce(grad_w_fc2, order_x)
        ((weight_fc2,),) = yield ("wait", [fetch_fc2])
        grad_hidden, grad_b_fc1 = rows_in(weight_fc2, grad_mlp, "slope", slope)
        grad_hidden = yield ("compute", grad_hidden, 9.0)
        grad_w_fc1 = weight_grad(mod_two, grad_hidden[None])
        grad_w_fc1 = yield ("compute", by_block(grad_w_fc1, grad_hidden.shape[0]), 5.0)
        sum_fc1 = reduce(grad_w_fc1, order_y)
        grad_mod_two = split_sum([(weight_fc1, grad_hidden)])
        grad_own = grad_all[:, :HALF].astype(f32)
        grad_after_cross = grad_own + norm_backward(
            grad_mod_two * (1.0 + scale_two), normed_two, inverse_two
        )
        grad_cross = join_cols(grad_after_cross.astype(bf16))
        grad_cross = yield ("compute", grad_cross, 26.0)

        grad_crossed = rows_in(weight_co, grad_cross).reshape(heads, HD, -1)
        grad_cq, *grad_kv = attend_grad(
            cross_q, text_k, text_v, grad_crossed, log_cross, length, True
        )
        grad_cq = yield ("compute", grad_cq, 11.0)
        grad_cq = grad_cq.reshape(half, -1)
        grad_kv = jnp.stack(grad_kv)[..., :TXT].reshape(2, half, TXT)
        captions_out = links.spawn(captions_out_task(grad_kv))
        grad_w_co = by_block(weight_grad(crossed, grad_cross.reshape(2, half, -1)), half)
        grad_w_cq = by_block(weight_grad(cross_in, grad_cq[None]), half)
        grad_w_cq = yield ("compute", grad_w_cq, 7.0)
        grad_after_self = grad_after_cross + split_sum([(weight_cq, grad_cq)])
        grad_branch = join_cols((gate_one * grad_after_self).astype(bf16))
        grad_branch = yield ("compute", grad_branch, 18.0)
        grad_attended = rows_in(weight_out, grad_branch).reshape(heads, HD, -1)
        grad_w_out = by_block(weight_grad(attended, grad_branch.reshape(2, half, -1)), half)
        grad_w_three = jnp.stack([grad_w_out, grad_w_co, grad_w_cq], axis=bits + 1)
        grad_w_three = yield ("compute", grad_w_three, 10.0)
        grad_attended = yield ("compute", grad_attended, 3.0)
        sum_three = reduce(grad_w_three, order_x)

        grad_q, grad_k, grad_v = attend_grad(
            queries, keys, values, grad_attended, log_self, length, False
        )
        grad_k = yield ("compute", grad_k, 17.0)
        grad_q, grad_k, grad_v = (g.reshape(half, -1) for g in (grad_q, grad_k, grad_v))
        grad_w_kv = jnp.stack(
            [by_block(weight_grad(mod_all, g[None]), half) for g in (grad_k, grad_v)],
            axis=bits + 1,
        )
        grad_w_kv = yield ("compute", grad_w_kv, 7.0)
        sum_kv = reduce(grad_w_kv, order_y)
        grad_w_q = by_block(weight_grad(mod_own, grad_q[None]), half)
        grad_w_q = yield ("compute", grad_w_q, 3.0)
        sum_q = reduce(grad_w_q, order_z)
        keep, send = rows_out([(weight_k, grad_k), (weight_v, grad_v), (weight_q, grad_q)])
        total = keep + swap(send, "col").astype(f32)
        total = yield ("compute", total, 16.0)
        far_part = yield (0, total[:, HALF:].astype(bf16))
        grad_mod_one = total[:, :HALF] + far_part.astype(f32)
        normed_one = (residual - mean_all[:, :HALF]) * inverse_all[:, :HALF]
        grad_latents = grad_after_self + norm_backward(
            grad_mod_one * (1.0 + scale_one), normed_one, inverse_all[:, :HALF]
        )
        latents_out = links.spawn(to_features(grad_latents.astype(bf16)))
        mlp_out = split_sum([(weight_fc2, activated)]) + bias_fc2
        result = (after_cross + gate_two * mlp_out).astype(bf16)
        result = yield ("compute", result, 12.0)
        result_out = links.spawn(to_features(result))

        ((grad_text, summed_ckv, grad_b_cv),) = yield ("wait", [captions_out])
        grad_vectors = jnp.concatenate(
            [
                jnp.sum(value, axis=1, keepdims=True)
                for value in (
                    grad_mod_one,
                    grad_mod_one * normed_one,
                    grad_after_self * branch,
                    grad_mod_two,
                    grad_mod_two * normed_two,
                    grad_own * mlp_out,
                    gate_one * grad_after_self,
                    grad_after_cross,
                    gate_two * grad_own,
                )
            ],
            axis=1,
        ).reshape(2, 2, quarter, 9)
        keep = lax.dynamic_index_in_dim(grad_vectors, c, 1, keepdims=False)
        sent = lax.dynamic_index_in_dim(grad_vectors, 1 - c, 1, keepdims=False)
        keep = (keep + swap(sent, "col")).transpose(0, 2, 1)
        col_grads = jnp.concatenate(
            [
                jnp.sum(grad_q.astype(f32), axis=1, keepdims=True),
                jnp.sum(grad_v.astype(f32), axis=1, keepdims=True),
                jnp.sum(grad_cq.astype(f32), axis=1, keepdims=True),
                0.5 * grad_b_cv,
            ],
            axis=1,
        )
        col_grads = jnp.concatenate(
            [
                col_grads.T.reshape(4, 2, quarter).transpose(1, 0, 2).reshape(2, -1),
                grad_b_fc1.reshape(2, -1),
            ],
            axis=1,
        )
        mine_cols = lax.dynamic_index_in_dim(col_grads, r, 0, keepdims=False)
        sent_cols = lax.dynamic_index_in_dim(col_grads, 1 - r, 0, keepdims=False)
        sent = jnp.concatenate([keep[1].reshape(-1), sent_cols])
        got = yield ("row", sent)
        got_wide = got[: 9 * quarter].reshape(9, quarter)
        own_wide = keep[0]
        latent_wide = jnp.stack([pick(own_wide, got_wide, r), pick(got_wide, own_wide, r)])
        mine_cols = mine_cols + got[9 * quarter :]
        flat = jnp.concatenate(
            [
                latent_wide[:, :6].reshape(-1),
                (own_wide + got_wide)[6:].reshape(-1),
                mine_cols,
            ]
        )
        flat = flat + (yield (0, flat))
        n_latent = LPP * 6 * quarter
        gathered, sums = flat[None, :n_latent], flat[n_latent:]
        for bit in range(1, bits):
            got = yield (bit, jnp.concatenate([gathered.reshape(-1), sums]))
            got_latents = got[: gathered.size].reshape(gathered.shape)
            sums = sums + got[gathered.size :]
            gathered = in_order(gathered, got_latents, (d >> bit) & 1, 0)
        gathered = gathered.reshape(-1, 6, quarter)
        grad_time_table = jnp.einsum(
            "ln,lkf->nkf", hot_of(time_ids), gathered, precision=lax.Precision.HIGHEST
        )
        wide_sums = sums[: 3 * quarter].reshape(3, quarter)
        col_sums = sums[3 * quarter :]

        waited = [sum_fc2, sum_fc1, sum_three, sum_kv, sum_q, latents_out, result_out]
        fc2, fc1, three, kv, sum_q, grad_latents, output = yield ("wait", waited)
        return (
            output,
            grad_latents.astype(f32),
            grad_text,
            grad_time_table,
            jnp.sum(gathered, axis=0),
            jnp.stack([sum_q, kv[0], kv[1]], axis=1),
            col_sums[: 2 * quarter].reshape(2, quarter),
            three[0],
            wide_sums[0],
            three[2],
            col_sums[2 * quarter : 3 * quarter],
            summed_ckv,
            col_sums[3 * quarter : 4 * quarter],
            three[1],
            wide_sums[1],
            fc1,
            col_sums[4 * quarter :],
            fc2,
            wide_sums[2],
        )

    def captions_out_task(grad_kv):
        far = yield (0, grad_kv)
        kv_sum = grad_kv.astype(f32) + far.astype(f32)
        grad_b_cv = jnp.sum(kv_sum[1], axis=1, keepdims=True)
        kv_latent = kv_sum.astype(bf16)
        kv_other = yield ("row", kv_latent)
        kv_own = pick(kv_latent, kv_other, r ^ upper)
        text_part = jnp.einsum("kot,iko->ti", kv_own, w_cross_kv, preferred_element_type=f32)
        text_quarter = text.shape[2]
        keep = pick(text_part[:, :text_quarter], text_part[:, text_quarter:], c)
        send = pick(text_part[:, text_quarter:], text_part[:, :text_quarter], c)
        grad_text = (keep + swap(send.astype(bf16), "col").astype(f32))[None]
        kv_all = lax.all_gather(kv_own, "dp")
        (text_rows,) = yield ("wait", [spread])
        summed_ckv = jnp.einsum(
            "lti,lkot->iko", text_rows, kv_all, preferred_element_type=f32
        )
        return grad_text, summed_ckv, grad_b_cv

    def hot_of(ids):
        return (ids[:, None] == jnp.arange(time_table.shape[0])[None, :]).astype(f32)

    text_row = in_order(text[0], swap(text[0], "col"), c, 1)
    text_block = 2 * text.shape[2] // n_dp
    text_mine = lax.dynamic_slice_in_dim(
        lax.all_gather(text[0], "dp"), d % (n_dp // 2) * text_block, text_block, 2
    )
    text_all = pick(text_mine, swap(text_mine, "col"), c ^ (d // (n_dp // 2)))
    length = lax.dynamic_slice_in_dim(text_len, my_latent, 1)

    latents_in = links.spawn(latents_in_task())
    q_k_v = w_qkv.transpose(1, 0, 2)
    fetch_kv = links.spawn(fetch(q_k_v, 1, 0, None, (q_k_v, 1), (q_k_v, 2)))
    vectors_in = links.spawn(vectors_in_task())
    fetch_q = links.spawn(fetch(q_k_v, 0, 1, None, (q_k_v, 0)))
    w_three = jnp.stack([w_out.T, w_cross_q, w_cross_out.T])
    fetch_three = links.spawn(fetch(w_three, 0, 1, fetch_kv, *((w_three, i) for i in range(3))))
    captions_in = links.spawn(captions_in_task())
    w_fc2_t = w_fc2.T
    fetch_fc1 = links.spawn(fetch(w_fc1[None], 0, 0, fetch_three, (w_fc1, None)))
    fetch_fc2 = links.spawn(fetch(w_fc2_t[None], 0, 1, fetch_fc1, (w_fc2_t, None)))
    spread = links.spawn(spread_task())
    grad_in = links.spawn(grad_out_task())
    main = links.spawn(main_task())
    links.run()
    return main.result


def solution(mesh):
    return jax.shard_map(
        local,
        mesh=mesh,
        in_specs=(
            P("dp", ("row", "col")),
            P("dp", None, ("row", "col")),
            P(),
            P(),
            P(None, None, ("row", "col")),
            P(None, ("row", "col")),
            P("row", None, "col"),
            P(None, ("col", "row")),
            P("col", "row"),
            P(("row", "col")),
            P("row", "col"),
            P(("col", "row")),
            P("row", None, "col"),
            P(("col", "row")),
            P("col", "row"),
            P(("row", "col")),
            P("row", "col"),
            P(("col", "row")),
            P("col", "row"),
            P(("row", "col")),
            P("dp", ("row", "col")),
        ),
        out_specs=(
            P("dp", ("row", "col")),
            P("dp", ("row", "col")),
            P("dp", None, ("row", "col")),
            P(None, None, ("row", "col")),
            P(None, ("row", "col")),
            P(("row", "dp"), None, "col"),
            P(None, ("col", "row")),
            P(("col", "dp"), "row"),
            P(("row", "col")),
            P(("row", "dp"), "col"),
            P(("col", "row")),
            P(("row", "dp"), None, "col"),
            P(("col", "row")),
            P(("col", "dp"), "row"),
            P(("row", "col")),
            P(("row", "dp"), "col"),
            P(("col", "row")),
            P(("col", "dp"), "row"),
            P(("row", "col")),
        ),
        check_vma=False,
    )
```

```python
from functools import partial

import jax
import jax.numpy as jnp
from jax import lax
from jax.experimental import pallas as pl
from jax.experimental.pallas import tpu as pltpu
from jax.sharding import PartitionSpec as P

HD = 72
TXT = 120
TXT_PAD = 128
SEQ_DEV = 512
LPP = 2
HALF = 256

norm_eps = 1e-06
masked_score = -1000000000.0
f32 = jnp.float32
bf16 = jnp.bfloat16
SMALL_COST = pl.CostEstimate(flops=1, bytes_accessed=1, transcendentals=0)


def swap(value, axis):
    return lax.ppermute(value, axis, [(0, 1), (1, 0)])


def swap_dp(value, bit):
    return lax.ppermute(value, "dp", [(i, i ^ (1 << bit)) for i in range(lax.axis_size("dp"))])


def pick(pair_first, pair_second, index):
    return jnp.where(index == 0, pair_first, pair_second)


def in_order(mine, other, index, axis):
    return jnp.concatenate([pick(mine, other, index), pick(other, mine, index)], axis=axis)


def after(value, *earlier):
    return lax.optimization_barrier((value, *earlier))[0]


def dot(left, right, left_dim, right_dim):
    return lax.dot_general(
        left, right, (((left_dim,), (right_dim,)), ((), ())), preferred_element_type=f32
    )


def scores_of(masked, length_ref, q, k):
    scores = dot(k, q, 0, 0) * (HD ** (-0.5))
    if masked:
        place = lax.broadcasted_iota(jnp.int32, scores.shape, 0)
        scores = jnp.where(place < length_ref[0], scores, masked_score)
    return scores


def attend_kernel(masked, length_ref, q_ref, k_ref, v_ref, o_ref, log_ref):
    scores = scores_of(masked, length_ref, q_ref[0], k_ref[0])
    largest = jnp.max(scores, axis=0, keepdims=True)
    raised = jnp.exp(scores - largest)
    total = jnp.sum(raised, axis=0, keepdims=True)
    mixture = dot(v_ref[0], raised.astype(bf16), 1, 0)
    o_ref[0] = (mixture / total).astype(bf16)
    log_ref[0] = largest + jnp.log(total)


def attend(q, k, v, length, masked):
    heads, hd, nq = q.shape
    nk = k.shape[2]
    head = lambda h: (h, 0, 0)
    return pl.pallas_call(
        partial(attend_kernel, masked),
        grid=(heads,),
        in_specs=[
            pl.BlockSpec(memory_space=pltpu.SMEM),
            pl.BlockSpec((1, hd, nq), head),
            pl.BlockSpec((1, hd, nk), head),
            pl.BlockSpec((1, hd, nk), head),
        ],
        out_specs=[pl.BlockSpec((1, hd, nq), head), pl.BlockSpec((1, 1, nq), head)],
        out_shape=[
            jax.ShapeDtypeStruct((heads, hd, nq), bf16),
            jax.ShapeDtypeStruct((heads, 1, nq), f32),
        ],
        compiler_params=pltpu.CompilerParams(vmem_limit_bytes=32 * 2**20),
        cost_estimate=SMALL_COST,
        name="attend_fwd",
    )(length, q, k, v)


def attend_grad_kernel(
    masked, length_ref, q_ref, k_ref, v_ref, g_ref, log_ref, dq_ref, dk_ref, dv_ref
):
    q, k, v, g = q_ref[0], k_ref[0], v_ref[0], g_ref[0]
    weights = jnp.exp(scores_of(masked, length_ref, q, k) - log_ref[0])
    grad_weights = dot(v, g, 0, 0)
    crossed = jnp.sum(grad_weights * weights, axis=0, keepdims=True)
    grad_scores = (weights * (grad_weights - crossed)).astype(bf16)
    dq_ref[0] = (dot(k, grad_scores, 1, 0) * (HD ** (-0.5))).astype(bf16)
    dk_ref[0] = (dot(q, grad_scores, 1, 1) * (HD ** (-0.5))).astype(bf16)
    dv_ref[0] = dot(g, weights.astype(bf16), 1, 1).astype(bf16)


def attend_grad(q, k, v, g, log_total, length, masked):
    heads, hd, nq = q.shape
    nk = k.shape[2]
    head = lambda h: (h, 0, 0)
    queries, keys = pl.BlockSpec((1, hd, nq), head), pl.BlockSpec((1, hd, nk), head)
    return pl.pallas_call(
        partial(attend_grad_kernel, masked),
        grid=(heads,),
        in_specs=[
            pl.BlockSpec(memory_space=pltpu.SMEM),
            queries,
            keys,
            keys,
            queries,
            pl.BlockSpec((1, 1, nq), head),
        ],
        out_specs=[queries, keys, keys],
        out_shape=[
            jax.ShapeDtypeStruct((heads, hd, nq), bf16),
            jax.ShapeDtypeStruct((heads, hd, nk), bf16),
            jax.ShapeDtypeStruct((heads, hd, nk), bf16),
        ],
        compiler_params=pltpu.CompilerParams(vmem_limit_bytes=40 * 2**20),
        cost_estimate=SMALL_COST,
        name="attend_bwd",
    )(length, q, k, v, g, log_total)


def assemble_kernel(kind, core_ref, mine_ref, other_ref, vectors_ref, *outs):
    quarter = mine_ref.shape[1]
    held = outs[-1]
    core = core_ref[0]
    for row in range(2):
        mine = pl.multiple_of((2 * row + core) * quarter, 16)
        other = pl.multiple_of((2 * row + 1 - core) * quarter, 16)
        held[pl.ds(mine, quarter), :] = mine_ref[row].astype(f32)
        held[pl.ds(other, quarter), :] = other_ref[row].astype(f32)
    state = held[...]
    if kind == "gate":
        outs[0][...] = state.astype(bf16)
        outs[1][...] = (state * vectors_ref[:, 5:6]).astype(bf16)
    else:
        mean = jnp.mean(state, axis=0, keepdims=True)
        center = state - mean
        inverse = lax.rsqrt(jnp.mean(center * center, axis=0, keepdims=True) + norm_eps)
        outs[0][...] = state.astype(bf16)
        scale, shift = 1.0 + vectors_ref[:, 1:2], vectors_ref[:, 0:1]
        outs[1][...] = (center * inverse * scale + shift).astype(bf16)
        outs[2][...] = mean
        outs[3][...] = inverse


def assemble(kind, mine, other, core, vectors):
    _, quarter, tokens = mine.shape
    features = 4 * quarter
    place = lambda t, core_ref: (0, 0, t - t % 2 + (t + core_ref[0]) % 2)
    columns = pl.BlockSpec(vectors.shape, lambda t, core_ref: (0, 0))
    block = pl.BlockSpec((features, HALF), lambda t, core_ref: (0, t))
    line = pl.BlockSpec((1, HALF), lambda t, core_ref: (0, t))
    outs, shapes = [block, block], [jax.ShapeDtypeStruct((features, tokens), bf16)] * 2
    if kind == "norm":
        outs, shapes = outs + [line] * 2, shapes + [jax.ShapeDtypeStruct((1, tokens), f32)] * 2
    return pl.pallas_call(
        partial(assemble_kernel, kind),
        grid_spec=pltpu.PrefetchScalarGridSpec(
            num_scalar_prefetch=1,
            grid=(tokens // HALF,),
            in_specs=[pl.BlockSpec((2, quarter, HALF), place)] * 2 + [columns],
            out_specs=outs,
            scratch_shapes=[pltpu.VMEM((features, HALF), f32)],
        ),
        out_shape=shapes,
        compiler_params=pltpu.CompilerParams(vmem_limit_bytes=32 * 2**20),
        cost_estimate=SMALL_COST,
        name="assemble_" + kind,
    )(core, mine, other, vectors)


class Weight:
    def __init__(self, pieces, places):
        self.arrays = [array for array, _ in pieces]
        self.leads = [lead for _, lead in pieces]
        self.rows = [array.shape[-2] for array in self.arrays]
        self.n = self.arrays[0].shape[-1]
        self.places = jnp.stack([jnp.asarray(place, jnp.int32) for place in places])

    def specs(self, cols, column):
        def spec(rows, lead):
            if lead is None:
                return pl.BlockSpec((rows, cols), lambda *grid: (0, column(*grid)))
            return pl.BlockSpec((None, rows, cols), lambda *grid: (lead, 0, column(*grid)))

        return [spec(rows, lead) for rows, lead in zip(self.rows, self.leads)]


def place_of(places_ref, index):
    return pl.multiple_of(places_ref[index], 16)


def gelu_parts(v):
    inner = 0.7978845608028654 * (v + 0.044715 * (v * v * v))
    bent = jnp.tanh(inner)
    slope = 0.7978845608028654 * (1.0 + 3 * 0.044715 * (v * v))
    return 0.5 * v * (1.0 + bent), 0.5 * (1.0 + bent) + 0.5 * v * (1.0 - bent * bent) * slope


def rows_in_kernel(count, kind, lane, places_ref, x_ref, *refs):
    pieces, rest = refs[:count], refs[count:]
    total = None
    for index, piece in enumerate(pieces):
        rows = x_ref[pl.ds(place_of(places_ref, index), piece.shape[0]), :]
        part = dot(piece[...], rows, 0, 0)
        total = part if total is None else total + part
    if kind == "plain":
        rest[0][...] = total.astype(bf16)
    elif kind == "bias":
        rest[1][...] = (total + rest[0][:, lane : lane + 1]).astype(bf16)
    elif kind == "gelu":
        value, slope = gelu_parts(total + rest[0][...])
        rest[1][...] = value.astype(bf16)
        rest[2][...] = slope.astype(bf16)
    elif kind == "slope":
        grad = total * rest[0][...].astype(f32)
        rest[1][...] = grad.astype(bf16)
        rest[2][...] = jnp.sum(grad, axis=1, keepdims=True)


def rows_in(weight, x, kind="plain", operand=None, lane=0):
    k, tokens = x.shape
    n = weight.n
    cols = 768 if n % 768 == 0 else n
    wide = min(tokens, 512)
    out_block = pl.BlockSpec((cols, wide), lambda i, t: (i, t))
    column = pl.BlockSpec((cols, 1), lambda i, t: (i, 0))
    out = jax.ShapeDtypeStruct((n, tokens), bf16)
    lanes = pl.BlockSpec((cols, operand.shape[1]), lambda i, t: (i, 0)) if kind == "bias" else None
    extra = {"plain": [], "bias": [lanes], "gelu": [column], "slope": [out_block]}[kind]
    specs, shapes = [out_block], [out]
    if kind == "gelu":
        specs, shapes = [out_block] * 2, [out] * 2
    if kind == "slope":
        specs, shapes = [out_block, column], [out, jax.ShapeDtypeStruct((n, 1), f32)]
    result = pl.pallas_call(
        partial(rows_in_kernel, len(weight.arrays), kind, lane),
        grid=(n // cols, tokens // wide),
        in_specs=[
            pl.BlockSpec(memory_space=pltpu.SMEM),
            pl.BlockSpec((k, wide), lambda i, t: (0, t)),
        ]
        + weight.specs(cols, lambda i, t: i)
        + extra,
        out_specs=specs,
        out_shape=shapes,
        compiler_params=pltpu.CompilerParams(vmem_limit_bytes=48 * 2**20),
        cost_estimate=SMALL_COST,
        name="rows_in_" + kind,
    )(weight.places, x, *weight.arrays, *([] if operand is None else [operand]))
    return result[0] if len(result) == 1 else result


def rows_out_kernel(counts, steps, *refs):
    sides = len(counts)
    places, ys = refs[:sides], refs[sides : 2 * sides]
    pieces, (keep_ref, send_ref) = refs[2 * sides : -2], refs[-2:]
    step = pl.program_id(0)

    def rows_of(side, index, piece):
        return pl.ds(place_of(places[side], index), piece.shape[0])

    def write(target, active):
        start = 0
        for side in range(sides):
            if side in active:
                for index, piece in enumerate(pieces[start : start + counts[side]]):
                    rows = rows_of(side, index, piece)
                    part = dot(piece[...], ys[side][...], 1, 0)
                    if side != active[0]:
                        part = part + target[rows, :].astype(f32)
                    target[rows, :] = part.astype(target.dtype)
            start += counts[side]

    for number in range(max(steps)):
        active = [side for side in range(sides) if number < steps[side]]

        @pl.when(step == number)
        def _():
            write(keep_ref if number % 2 == 0 else send_ref, active)


def rows_out(pairs):
    k = 2 * pairs[0][0].rows[0]
    steps = [y.shape[1] // HALF for _, y in pairs]
    most = max(steps)

    def y_spec(y, count):
        return pl.BlockSpec((y.shape[0], HALF), lambda t: (0, jnp.minimum(t, count - 1)))

    in_specs = [pl.BlockSpec(memory_space=pltpu.SMEM) for _ in pairs]
    in_specs += [y_spec(y, count) for (_, y), count in zip(pairs, steps)]
    operands = [w.places for w, _ in pairs] + [y for _, y in pairs]
    for w, _ in pairs:
        in_specs += w.specs(w.n, lambda t: 0)
        operands += w.arrays
    width = most // 2 * HALF
    out_block = pl.BlockSpec((k, HALF), lambda t: (0, t // 2))
    return pl.pallas_call(
        partial(rows_out_kernel, [len(w.arrays) for w, _ in pairs], steps),
        grid=(most,),
        in_specs=in_specs,
        out_specs=[out_block, out_block],
        out_shape=[jax.ShapeDtypeStruct((k, width), f32), jax.ShapeDtypeStruct((k, width), bf16)],
        compiler_params=pltpu.CompilerParams(vmem_limit_bytes=48 * 2**20),
        cost_estimate=SMALL_COST,
        name="rows_out",
    )(*operands)


def weight_grad_kernel(inputs_ref, grads_ref, out_ref):
    out_ref[0] = dot(inputs_ref[...], grads_ref[0], 1, 1).astype(bf16)


def weight_grad(inputs, grads, first=0, groups=None):
    k, tokens = inputs.shape
    total, n, _ = grads.shape
    groups = total if groups is None else groups
    rows = 384 if k % 384 == 0 else 288
    return pl.pallas_call(
        weight_grad_kernel,
        grid=(groups, k // rows),
        in_specs=[
            pl.BlockSpec((rows, tokens), lambda g, i: (i, 0)),
            pl.BlockSpec((1, n, tokens), lambda g, i: (first + g, 0, 0)),
        ],
        out_specs=pl.BlockSpec((1, rows, n), lambda g, i: (g, i, 0)),
        out_shape=jax.ShapeDtypeStruct((groups, k, n), bf16),
        compiler_params=pltpu.CompilerParams(vmem_limit_bytes=40 * 2**20),
        cost_estimate=SMALL_COST,
        name="weight_grad",
    )(inputs, grads)


def norm_forward(state):
    center = state - jnp.mean(state, axis=0, keepdims=True)
    inverse = lax.rsqrt(jnp.mean(center * center, axis=0, keepdims=True) + norm_eps)
    return (center * inverse, inverse)


def norm_backward(grad_normed, normed, inverse):
    return inverse * (
        grad_normed
        - jnp.mean(grad_normed, axis=0, keepdims=True)
        - normed * jnp.mean(grad_normed * normed, axis=0, keepdims=True)
    )


def split_sum(pairs):
    keep, send = rows_out(pairs)
    return keep + swap(send, "col").astype(f32)


def join_cols(own):
    return jnp.concatenate([own, swap(own, "col")], axis=1)


def reduce_pieces(held, order, dp_index):
    bits = lax.axis_size("dp").bit_length() - 1
    left = ["row"] + list(range(bits - 1, -1, -1))
    for step, name in enumerate(order):
        axis = left.index(name)
        if name == "row":
            keep = lax.index_in_dim(held, 0, axis, keepdims=False)
            send = lax.index_in_dim(held, 1, axis, keepdims=False)
        else:
            bit = (dp_index >> name) & 1
            keep = lax.dynamic_index_in_dim(held, bit, axis, keepdims=False)
            send = lax.dynamic_index_in_dim(held, 1 - bit, axis, keepdims=False)
        got = yield (name, send)
        left.pop(axis)
        held = keep.astype(f32) + got.astype(f32)
        if step < len(order) - 1:
            held = held.astype(bf16)
    return held


class Task:
    def __init__(self, steps):
        self.steps, self.done, self.result, self.half = steps, False, None, None


class Links:
    def __init__(self):
        self.free, self.events, self.waits = {}, [], []
        self.rate = 138e3
        self.last, self.now, self.count, self.halves = None, 0.0, 0, []

    def push(self, time, task, got, tie):
        self.count += 1
        self.events.append((time, self.count, task, got, tie))

    def spawn(self, steps):
        task = Task(steps)
        self.push(self.now, task, None, False)
        return task

    def ask(self, task, request):
        kind = request[0]
        if kind == "wait":
            self.waits.append((task, request[1]))
            return
        if kind == "half":
            self.halves.append((task, request[1]))
            return
        if kind == "set":
            task.half = request[1]
            self.push(self.now, task, None, False)
            return
        if kind == "compute":
            end = max(self.now, self.free.get("compute", 0.0)) + request[2]
            self.free["compute"] = end
            self.push(end, task, request[1], True)
            return
        value = request[1]
        link = {"row": "x", 0: "y"}.get(kind, "z")
        hops = 2 ** max(kind - 1, 0) if isinstance(kind, int) else 1
        end = max(self.now, self.free.get(link, 0.0)) + 2.0
        end += hops * value.size * value.dtype.itemsize / self.rate
        self.free[link] = end
        got = swap_dp(value, kind) if isinstance(kind, int) else swap(value, kind)
        self.push(end, task, got, True)

    def run(self):
        while self.events:
            event = min(self.events, key=lambda item: item[:2])
            self.events.remove(event)
            self.now, _, task, got, tie = event
            if tie:
                if self.last is not None:
                    got = after(got, self.last)
                self.last = got
            try:
                self.ask(task, task.steps.send(got))
            except StopIteration as stop:
                task.done, task.result = True, stop.value
            still = []
            for waiting, others in self.waits:
                if all(other.done for other in others):
                    self.push(self.now, waiting, [other.result for other in others], False)
                else:
                    still.append((waiting, others))
            self.waits = still
            for waiting, other in [pair for pair in self.halves if pair[1].half is not None]:
                self.halves.remove((waiting, other))
                self.push(self.now, waiting, None, False)


def local(
    latents,
    text,
    text_len,
    time_ids,
    time_table,
    shift_table,
    w_qkv,
    b_qv,
    w_out,
    b_out,
    w_cross_q,
    b_cross_q,
    w_cross_kv,
    b_cross_v,
    w_cross_out,
    b_cross_out,
    w_fc1,
    b_fc1,
    w_fc2,
    b_fc2,
    grad_out,
):
    quarter = latents.shape[1]
    half = 2 * quarter
    heads = half // HD
    n_dp = lax.axis_size("dp")
    bits = n_dp.bit_length() - 1
    d = lax.axis_index("dp")
    r = lax.axis_index("row")
    c = lax.axis_index("col")
    upper = d % 2
    pair = d // 2
    my_latent = pair * LPP + r

    def own_and_sent(values):
        turned = values.T
        return tuple(
            lax.dynamic_slice_in_dim(turned, place * SEQ_DEV, SEQ_DEV, 1) for place in (r, 1 - r)
        )

    links = Links()
    core = c[None].astype(jnp.int32)

    def fetch(blocks, first, bit, behind, *choices):
        w, (rows, n) = len(choices), blocks.shape[1:]
        if behind is not None:
            yield ("half", behind)
            blocks = after(blocks, behind.half)
        mine = (d >> bit) & 1
        half_rows = rows // 2
        got = yield (
            "row",
            lax.dynamic_slice(blocks, (first, mine * half_rows, 0), (w, half_rows, n)),
        )
        yield ("set", got)
        relayed = yield (bit, got)
        more = [(got, rows + half_rows * mine), (relayed, rows + half_rows * (1 - mine))]
        return [
            Weight([own] + [(array, i) for array, _ in more], [0] + [place for _, place in more])
            for i, own in enumerate(choices)
        ]

    def near_task(values):
        own, sent = own_and_sent(values)
        return jnp.stack([own, (yield ("row", sent))])

    def latents_in_task():
        near = yield from near_task(latents)
        far = yield (0, near)
        both = jnp.concatenate([near, far], axis=-1)
        return both, swap(both, "col")

    def grad_out_task():
        near = yield from near_task(grad_out)
        return near, swap(near, "col")

    def vectors_in_task():
        pair_times = lax.dynamic_slice_in_dim(time_ids, pair * LPP, LPP)
        one_hot = hot_of(pair_times)
        modulation = shift_table[None] + jnp.einsum(
            "ln,nkf->lkf", one_hot, time_table, precision=lax.Precision.HIGHEST
        )
        feature_biases = jnp.stack([b_out, b_cross_out, b_fc2])
        wide = jnp.concatenate(
            [modulation, jnp.broadcast_to(feature_biases, (LPP, 3, quarter))], axis=1
        )
        col_biases = jnp.concatenate([b_qv.reshape(-1), b_cross_q, b_cross_v, b_fc1])
        got = yield (
            "row",
            jnp.concatenate([pick(wide[1], wide[0], r).reshape(-1), col_biases]),
        )
        wide_rows = jnp.stack(
            [pick(wide[0], wide[1], r), got[: 9 * quarter].reshape(9, quarter)]
        )
        wide_other = swap(wide_rows, "col")
        wide_all = jnp.stack(
            [pick(wide_rows, wide_other, c), pick(wide_other, wide_rows, c)], axis=1
        )
        vectors = wide_all.transpose(0, 1, 3, 2).reshape(2 * half, 9)
        got_cols = got[9 * quarter :]
        four, four_got = (v[: 4 * quarter].reshape(4, quarter) for v in (col_biases, got_cols))
        fc1 = in_order(col_biases[4 * quarter :], got_cols[4 * quarter :], r, 0)[:, None]
        return vectors, in_order(four, four_got, r, 1).T, fc1

    def spread_task():
        yield ("wait", [fetch_three])
        return (yield ("compute", text_all, 0.0))

    def captions_in_task():
        ((_, cols, _),) = yield ("wait", [vectors_in])
        kv_part = jnp.einsum("ti,iko->kot", text_row, w_cross_kv, preferred_element_type=f32)
        far = yield ("row", kv_part.astype(bf16))
        kv_total = kv_part + far.astype(f32)
        kv_total = jnp.concatenate(
            [kv_total[0].astype(bf16), (kv_total[1] + cols[:, 3:]).astype(bf16)]
        )
        kv_far = yield (0, kv_total)
        kv_mine = pick(kv_total, kv_far, r ^ upper).reshape(2, heads, HD, TXT)
        kv_mine = jnp.pad(kv_mine, ((0, 0), (0, 0), (0, 0), (0, TXT_PAD - TXT)))
        return kv_mine[0], kv_mine[1]

    dp_bits = list(range(bits))
    rest = dp_bits[2:]
    order_fc2 = ["row", 0, 1] + rest
    order_fc1 = ([0, 1, "row"] + rest, [1, 0, "row"] + rest)
    order_three = [0, 1, "row"] + rest
    order_kv = ["row", 0, 1] + rest
    order_q = [1, "row", 0] + rest

    def by_block(grads, n):
        return grads.reshape((2,) + (2,) * bits + (-1, n))

    def reduce(grads, order):
        return links.spawn(reduce_pieces(grads, order, d))

    def to_features(own):
        blocks = own.reshape(2, 2, quarter, HALF)
        keep = lax.dynamic_index_in_dim(blocks, c, 1, keepdims=False)
        got = swap(lax.dynamic_index_in_dim(blocks, 1 - c, 1, keepdims=False), "col")
        tokens = in_order(keep, got, c, 2)
        other = yield ("row", tokens[1])
        return in_order(tokens[0], other, r, 1).T

    def main_task():
        ((lat_both, lat_other), (vectors, biases, bias_fc1)) = yield (
            "wait",
            [latents_in, vectors_in],
        )
        shift_one, scale_one, gate_one, shift_two, scale_two, gate_two = (
            vectors[:, i : i + 1] for i in range(6)
        )
        bias_out, bias_co, bias_fc2 = (vectors[:, i : i + 1] for i in range(6, 9))
        lat_all, mod_all, mean_all, inverse_all = assemble(
            "norm", lat_both, lat_other, core, vectors
        )
        mod_all = yield ("compute", mod_all, 6.0)
        mod_own = mod_all[:, :SEQ_DEV]
        ((weight_k, weight_v),) = yield ("wait", [fetch_kv])
        keys = rows_in(weight_k, mod_all).reshape(heads, HD, -1)
        values = rows_in(weight_v, mod_all, "bias", biases, 1).reshape(heads, HD, -1)
        values = yield ("compute", values, 8.0)
        ((weight_q,),) = yield ("wait", [fetch_q])
        queries = rows_in(weight_q, mod_own, "bias", biases, 0).reshape(heads, HD, -1)
        attended, log_self = attend(queries, keys, values, length, False)
        attended = yield ("compute", attended, 13.0)
        attended = attended.reshape(half, -1)
        ((weight_out, weight_cq, weight_co),) = yield ("wait", [fetch_three])
        branch = split_sum([(weight_out, attended)]) + bias_out
        residual = lat_all[:, :HALF].astype(f32)
        after_self = residual + gate_one * branch
        cross_in = join_cols(after_self.astype(bf16))
        cross_in = yield ("compute", cross_in, 12.0)

        ((text_k, text_v),) = yield ("wait", [captions_in])
        cross_q = rows_in(weight_cq, cross_in, "bias", biases, 2).reshape(heads, HD, -1)
        crossed, log_cross = attend(cross_q, text_k, text_v, length, True)
        crossed = yield ("compute", crossed, 8.0)
        crossed = crossed.reshape(half, -1)
        after_cross = after_self + split_sum([(weight_co, crossed)]) + bias_co

        normed_two, inverse_two = norm_forward(after_cross)
        mod_two = join_cols((normed_two * (1.0 + scale_two) + shift_two).astype(bf16))
        mod_two = yield ("compute", mod_two, 15.0)
        ((weight_fc1,),) = yield ("wait", [fetch_fc1])
        activated, slope = rows_in(weight_fc1, mod_two, "gelu", bias_fc1)
        activated = yield ("compute", activated, 10.0)
        links.rate = 46e3

        ((grad_near, grad_other),) = yield ("wait", [grad_in])
        grad_all, grad_mlp = assemble("gate", grad_near, grad_other, core, vectors)
        grad_w_fc2 = by_block(weight_grad(activated, grad_mlp.reshape(2, half, -1)), half)
        grad_w_fc2 = yield ("compute", grad_w_fc2, 9.0)
        sum_fc2 = reduce(grad_w_fc2, order_fc2)
        ((weight_fc2,),) = yield ("wait", [fetch_fc2])
        grad_hidden, grad_b_fc1 = rows_in(weight_fc2, grad_mlp, "slope", slope)
        grad_hidden = yield ("compute", grad_hidden, 9.0)
        ff_half = grad_hidden.shape[0] // 2
        split = grad_hidden.reshape(2, ff_half, -1)
        sum_fc1 = []
        for i, order in enumerate(order_fc1):
            grad_w_fc1 = by_block(weight_grad(mod_two, split, i, 1), ff_half)
            grad_w_fc1 = yield ("compute", grad_w_fc1, 3.0)
            sum_fc1.append(reduce(grad_w_fc1, order))
        grad_mod_two = split_sum([(weight_fc1, grad_hidden)])
        grad_own = grad_all[:, :HALF].astype(f32)
        grad_after_cross = grad_own + norm_backward(
            grad_mod_two * (1.0 + scale_two), normed_two, inverse_two
        )
        grad_cross = join_cols(grad_after_cross.astype(bf16))
        grad_cross = yield ("compute", grad_cross, 26.0)

        grad_crossed = rows_in(weight_co, grad_cross).reshape(heads, HD, -1)
        grad_cq, *grad_kv = attend_grad(
            cross_q, text_k, text_v, grad_crossed, log_cross, length, True
        )
        grad_cq = yield ("compute", grad_cq, 11.0)
        grad_cq = grad_cq.reshape(half, -1)
        grad_kv = jnp.stack(grad_kv)[..., :TXT].reshape(2, half, TXT)
        captions_out = links.spawn(captions_out_task(grad_kv))
        grad_w_co = by_block(weight_grad(crossed, grad_cross.reshape(2, half, -1)), half)
        grad_w_cq = by_block(weight_grad(cross_in, grad_cq[None]), half)
        grad_w_cq = yield ("compute", grad_w_cq, 7.0)
        grad_after_self = grad_after_cross + split_sum([(weight_cq, grad_cq)])
        grad_branch = join_cols((gate_one * grad_after_self).astype(bf16))
        grad_branch = yield ("compute", grad_branch, 18.0)
        grad_attended = rows_in(weight_out, grad_branch).reshape(heads, HD, -1)
        grad_w_out = by_block(weight_grad(attended, grad_branch.reshape(2, half, -1)), half)
        grad_w_three = jnp.stack([grad_w_out, grad_w_co, grad_w_cq], axis=bits + 1)
        grad_w_three = yield ("compute", grad_w_three, 10.0)
        grad_attended = yield ("compute", grad_attended, 3.0)
        sum_three = reduce(grad_w_three, order_three)

        grad_q, grad_k, grad_v = attend_grad(
            queries, keys, values, grad_attended, log_self, length, False
        )
        grad_k = yield ("compute", grad_k, 17.0)
        grad_q, grad_k, grad_v = (g.reshape(half, -1) for g in (grad_q, grad_k, grad_v))
        grad_w_kv = jnp.stack(
            [by_block(weight_grad(mod_all, g[None]), half) for g in (grad_k, grad_v)],
            axis=bits + 1,
        )
        grad_w_kv = yield ("compute", grad_w_kv, 7.0)
        sum_kv = reduce(grad_w_kv, order_kv)
        grad_w_q = by_block(weight_grad(mod_own, grad_q[None]), half)
        grad_w_q = yield ("compute", grad_w_q, 3.0)
        sum_q = reduce(grad_w_q, order_q)
        keep, send = rows_out([(weight_k, grad_k), (weight_v, grad_v), (weight_q, grad_q)])
        total = keep + swap(send, "col").astype(f32)
        total = yield ("compute", total, 16.0)
        far_part = yield (0, total[:, HALF:].astype(bf16))
        grad_mod_one = total[:, :HALF] + far_part.astype(f32)
        normed_one = (residual - mean_all[:, :HALF]) * inverse_all[:, :HALF]
        grad_latents = grad_after_self + norm_backward(
            grad_mod_one * (1.0 + scale_one), normed_one, inverse_all[:, :HALF]
        )
        latents_out = links.spawn(to_features(grad_latents.astype(bf16)))
        mlp_out = split_sum([(weight_fc2, activated)]) + bias_fc2
        result = (after_cross + gate_two * mlp_out).astype(bf16)
        result = yield ("compute", result, 12.0)
        result_out = links.spawn(to_features(result))

        ((grad_text, summed_ckv, grad_b_cv),) = yield ("wait", [captions_out])
        grad_vectors = jnp.concatenate(
            [
                jnp.sum(value, axis=1, keepdims=True)
                for value in (
                    grad_mod_one,
                    grad_mod_one * normed_one,
                    grad_after_self * branch,
                    grad_mod_two,
                    grad_mod_two * normed_two,
                    grad_own * mlp_out,
                    gate_one * grad_after_self,
                    grad_after_cross,
                    gate_two * grad_own,
                )
            ],
            axis=1,
        ).reshape(2, 2, quarter, 9)
        keep = lax.dynamic_index_in_dim(grad_vectors, c, 1, keepdims=False)
        sent = lax.dynamic_index_in_dim(grad_vectors, 1 - c, 1, keepdims=False)
        keep = (keep + swap(sent, "col")).transpose(0, 2, 1)
        col_grads = jnp.concatenate(
            [
                jnp.sum(grad_q.astype(f32), axis=1, keepdims=True),
                jnp.sum(grad_v.astype(f32), axis=1, keepdims=True),
                jnp.sum(grad_cq.astype(f32), axis=1, keepdims=True),
                0.5 * grad_b_cv,
            ],
            axis=1,
        )
        col_grads = jnp.concatenate(
            [
                col_grads.T.reshape(4, 2, quarter).transpose(1, 0, 2).reshape(2, -1),
                grad_b_fc1.reshape(2, -1),
            ],
            axis=1,
        )
        mine_cols = lax.dynamic_index_in_dim(col_grads, r, 0, keepdims=False)
        sent_cols = lax.dynamic_index_in_dim(col_grads, 1 - r, 0, keepdims=False)
        sent = jnp.concatenate([keep[1].reshape(-1), sent_cols])
        got = yield ("row", sent)
        got_wide = got[: 9 * quarter].reshape(9, quarter)
        own_wide = keep[0]
        latent_wide = jnp.stack([pick(own_wide, got_wide, r), pick(got_wide, own_wide, r)])
        mine_cols = mine_cols + got[9 * quarter :]
        flat = jnp.concatenate(
            [
                latent_wide[:, :6].reshape(-1),
                (own_wide + got_wide)[6:].reshape(-1),
                mine_cols,
            ]
        )
        flat = flat + (yield (0, flat))
        n_latent = LPP * 6 * quarter
        gathered, sums = flat[None, :n_latent], flat[n_latent:]
        for bit in range(1, bits):
            got = yield (bit, jnp.concatenate([gathered.reshape(-1), sums]))
            got_latents = got[: gathered.size].reshape(gathered.shape)
            sums = sums + got[gathered.size :]
            gathered = in_order(gathered, got_latents, (d >> bit) & 1, 0)
        gathered = gathered.reshape(-1, 6, quarter)
        grad_time_table = jnp.einsum(
            "ln,lkf->nkf", hot_of(time_ids), gathered, precision=lax.Precision.HIGHEST
        )
        wide_sums = sums[: 3 * quarter].reshape(3, quarter)
        col_sums = sums[3 * quarter :]

        waited = [sum_fc2, *sum_fc1, sum_three, sum_kv, sum_q, latents_out, result_out]
        fc2, fc1_a, fc1_b, three, kv, sum_q, grad_latents, output = yield ("wait", waited)
        return (
            output,
            grad_latents.astype(f32),
            grad_text,
            grad_time_table,
            jnp.sum(gathered, axis=0),
            jnp.stack([sum_q, kv[0], kv[1]], axis=1),
            col_sums[: 2 * quarter].reshape(2, quarter),
            three[0],
            wide_sums[0],
            three[2],
            col_sums[2 * quarter : 3 * quarter],
            summed_ckv,
            col_sums[3 * quarter : 4 * quarter],
            three[1],
            wide_sums[1],
            jnp.concatenate([fc1_a, fc1_b], axis=1),
            col_sums[4 * quarter :],
            fc2,
            wide_sums[2],
        )

    def captions_out_task(grad_kv):
        far = yield (0, grad_kv)
        kv_sum = grad_kv.astype(f32) + far.astype(f32)
        grad_b_cv = jnp.sum(kv_sum[1], axis=1, keepdims=True)
        kv_latent = kv_sum.astype(bf16)
        kv_other = yield ("row", kv_latent)
        kv_own = pick(kv_latent, kv_other, r ^ upper)
        text_part = jnp.einsum("kot,iko->ti", kv_own, w_cross_kv, preferred_element_type=f32)
        text_quarter = text.shape[2]
        keep = pick(text_part[:, :text_quarter], text_part[:, text_quarter:], c)
        send = pick(text_part[:, text_quarter:], text_part[:, :text_quarter], c)
        grad_text = (keep + swap(send.astype(bf16), "col").astype(f32))[None]
        kv_all = lax.all_gather(kv_own, "dp")
        (text_rows,) = yield ("wait", [spread])
        summed_ckv = jnp.einsum(
            "lti,lkot->iko", text_rows, kv_all, preferred_element_type=f32
        )
        return grad_text, summed_ckv, grad_b_cv

    def hot_of(ids):
        return (ids[:, None] == jnp.arange(time_table.shape[0])[None, :]).astype(f32)

    text_row = in_order(text[0], swap(text[0], "col"), c, 1)
    text_block = 2 * text.shape[2] // n_dp
    text_mine = lax.dynamic_slice_in_dim(
        lax.all_gather(text[0], "dp"), d % (n_dp // 2) * text_block, text_block, 2
    )
    text_all = pick(text_mine, swap(text_mine, "col"), c ^ (d // (n_dp // 2)))
    length = lax.dynamic_slice_in_dim(text_len, my_latent, 1)

    latents_in = links.spawn(latents_in_task())
    q_k_v = w_qkv.transpose(1, 0, 2)
    fetch_kv = links.spawn(fetch(q_k_v, 1, 0, None, (q_k_v, 1), (q_k_v, 2)))
    vectors_in = links.spawn(vectors_in_task())
    fetch_q = links.spawn(fetch(q_k_v, 0, 1, None, (q_k_v, 0)))
    w_three = jnp.stack([w_out.T, w_cross_q, w_cross_out.T])
    fetch_three = links.spawn(fetch(w_three, 0, 1, fetch_kv, *((w_three, i) for i in range(3))))
    captions_in = links.spawn(captions_in_task())
    w_fc2_t = w_fc2.T
    fetch_fc1 = links.spawn(fetch(w_fc1[None], 0, 0, fetch_three, (w_fc1, None)))
    fetch_fc2 = links.spawn(fetch(w_fc2_t[None], 0, 1, fetch_fc1, (w_fc2_t, None)))
    spread = links.spawn(spread_task())
    grad_in = links.spawn(grad_out_task())
    main = links.spawn(main_task())
    links.run()
    return main.result


def solution(mesh):
    return jax.shard_map(
        local,
        mesh=mesh,
        in_specs=(
            P("dp", ("row", "col")),
            P("dp", None, ("row", "col")),
            P(),
            P(),
            P(None, None, ("row", "col")),
            P(None, ("row", "col")),
            P("row", None, "col"),
            P(None, ("col", "row")),
            P("col", "row"),
            P(("row", "col")),
            P("row", "col"),
            P(("col", "row")),
            P("row", None, "col"),
            P(("col", "row")),
            P("col", "row"),
            P(("row", "col")),
            P("row", "col"),
            P(("col", "row")),
            P("col", "row"),
            P(("row", "col")),
            P("dp", ("row", "col")),
        ),
        out_specs=(
            P("dp", ("row", "col")),
            P("dp", ("row", "col")),
            P("dp", None, ("row", "col")),
            P(None, None, ("row", "col")),
            P(None, ("row", "col")),
            P(("row", "dp"), None, "col"),
            P(None, ("col", "row")),
            P(("col", "dp"), "row"),
            P(("row", "col")),
            P(("row", "dp"), "col"),
            P(("col", "row")),
            P(("row", "dp"), None, "col"),
            P(("col", "row")),
            P(("col", "dp"), "row"),
            P(("row", "col")),
            P(("row", "dp"), "col"),
            P(("col", "row")),
            P(("col", "dp"), "row"),
            P(("row", "col")),
        ),
        check_vma=False,
    )
```
